512 devices in a mesh: chan: 16 (over z_lo, x, core), slab: 32 (over y, z_hi).
Axes of the slice: x: 4, y: 8, z: 8 (z_hi: 4, z_lo: 2; z = z_hi * 2 + z_lo), core: 2. Of those that a mesh axis runs over, the one named last changes fastest.
Arguments:
- image: float32 [16, 1024, 1024], P('chan', 'slab'), may hold values from 0 to 2
- margin: int32 [32], P('slab'), may hold values from 1 to 3
- cells: int32 [16, 131072], P('chan', 'slab'), may hold values from 1 to 32767
- weights: float32 [16, 131072], P('chan', 'slab'), may hold values from 0.25 to 4
- observed: float32 [2, 16, 131072], P(None, 'chan', 'slab'), may hold values from -6 to 6
- dual_start: float32 [2, 16, 131072], P(None, 'chan', 'slab'), may hold values from -4 to 4
Outputs:
- restored: float32 [16, 1024, 1024], P('chan', 'slab')
- vis_dual: float32 [2, 16, 131072], P(None, 'chan', 'slab')
The draws below stay inside these ranges and needn't reach their ends.
Inputs may be any that keep to these rules, and one draw needn't show every extreme that they name: `cells`: visibility k of a channel belongs to facet s = k div 4096; its value q names frequency column s * 32 + q div 1024 and frequency row q mod 1024.
All inputs are finite; a program needn't handle non-finite values.
Results may differ from the reference program's by a relative error of at most 0.0047.
Values may be sent and summed in bfloat16 or wider, within the bound.
No kernel may reach another device: no remote copies, remote signals or barrier semaphores. Data moves between devices by JAX's collectives and lax.ppermute only.
A program may use at most 64 MiB of HBM per device.

```python
import math
import jax
import jax.numpy as jnp
from jax import lax

N = 1024
VIS_DEV = 4096
ITERS = 1
HALO = 3
CHANNELS = 16
FACETS = 32
ROWS_DEV = 32
VISIBILITIES = 131072


def place_ends(result, stream_key, smallest, top_value):
    longest = result.shape.index(max(result.shape))
    spots = []
    for shift in (0, 1):
        where = [jax.random.randint(jax.random.fold_in(stream_key, axis), (), 0, length) for axis, length in enumerate(result.shape)]
        where[longest] = (where[longest] + shift) % result.shape[longest]
        spots.append(tuple(where))
    return result.at[spots[0]].set(smallest).at[spots[1]].set(top_value)


def block_scale(key, dims, shards, smallest, high):
    loudness = 1.0
    for dim, blocks in shards:
        steps = jax.random.uniform(jax.random.fold_in(jax.random.fold_in(key, 6), dim), (blocks,), jnp.float32, smallest / len(shards), high / len(shards))
        loudness = loudness * jnp.repeat(jnp.exp(steps), dims[dim] // blocks).reshape((-1,) + (1,) * (len(dims) - 1 - dim))
    return loudness


def scatter_about(stream_key, dims, scale, reach, split=(), kind=jnp.bfloat16):
    level = block_scale(stream_key, dims, split, -0.22, 0.18) if split else 1.0
    entries = jax.random.normal(stream_key, dims, jnp.float32) * scale * level
    return jnp.minimum(jnp.maximum(entries, -reach), reach).astype(kind)


def setup_inputs(seed: int = 0) -> dict:
    splits = jax.random.split(jax.random.key(seed), 7)
    return {
        "image": jnp.clip(2.0 * jax.random.uniform(splits[0], (CHANNELS, N, N), jnp.float32) ** block_scale(splits[0], (CHANNELS, N, N), ((0, 16), (1, 32)), -0.2, 0.2), 0.0, 2.0),
        "margin": place_ends(jax.random.randint(splits[1], (FACETS,), 1, HALO + 1), jax.random.fold_in(splits[1], 1), 1, HALO).astype(jnp.int32),
        "cells": place_ends(jax.random.randint(splits[2], (CHANNELS, VISIBILITIES), 1, ROWS_DEV * N), jax.random.fold_in(splits[2], 1), 1, (ROWS_DEV * N) - 1).astype(jnp.int32),
        "weights": jnp.clip(jnp.exp(math.log(4.0) - 2.7725887 * jax.random.uniform(splits[3], (CHANNELS, VISIBILITIES), jnp.float32) ** block_scale(splits[3], (CHANNELS, VISIBILITIES), ((0, 16), (1, 32)), -0.2, 0.2)), 0.25, 4.0),
        "observed": scatter_about(splits[4], (2, CHANNELS, VISIBILITIES), 1.0, 6.0, ((1, 16), (2, 32)), jnp.float32),
        "dual_start": scatter_about(splits[5], (2, CHANNELS, VISIBILITIES), 0.5, 4.0, ((1, 16), (2, 32)), jnp.float32),
    }


low_taps = (-0.010597401784997278, 0.032883011666982945, 0.030841381835986965, -0.18703481171888114, -0.02798376941698385, 0.6308807679295904, 0.7148465705525415, 0.23037781330885523)
high_taps = (-0.23037781330885523, 0.7148465705525415, -0.6308807679295904, -0.02798376941698385, 0.18703481171888114, 0.030841381835986965, -0.032883011666982945, -0.010597401784997278)
tau_step = 0.5
bound_level = 3.0

def tap_value(offset, taps):
    total = jnp.zeros(offset.shape, jnp.float32)
    for position in range(8):
        total = total + jnp.where(offset == position, taps[position], 0.0).astype(jnp.float32)
    return total

def fourier_tables(length):
    index = jnp.arange(length, dtype=jnp.int32)
    product = index[:, None] * index[None, :] % length
    angle = product.astype(jnp.float32) * (2.0 * math.pi / length)
    scale = 1.0 / math.sqrt(length)
    return ((jnp.cos(angle) * scale).astype(jnp.bfloat16), (jnp.sin(angle) * scale).astype(jnp.bfloat16))

def column_matrix(length):
    half = length // 2
    line = jnp.arange(length, dtype=jnp.int32)[:, None]
    column = jnp.arange(length, dtype=jnp.int32)[None, :]
    offset = line - 2 * (column % half) + HALO
    return jnp.where(column < half, tap_value(offset, low_taps), tap_value(offset, high_taps))

def row_matrix(count):
    half = count // 2
    line = jnp.arange(count + 2 * HALO, dtype=jnp.int32)[:, None]
    column = jnp.arange(count, dtype=jnp.int32)[None, :]
    offset = line - 2 * (column % half)
    return jnp.where(column < half, tap_value(offset, low_taps), tap_value(offset, high_taps))

def facet_mask(count, width):
    line = jnp.arange(count + 2 * HALO, dtype=jnp.int32)
    distance = jnp.maximum(jnp.maximum(HALO - line, line - count - HALO + 1), 0)
    return (distance[None, :] <= width[:, None]).astype(jnp.float32)

def forward_grid(plane, cos_table, sin_table):
    flat_b = plane.astype(jnp.bfloat16)
    spec_real = jnp.dot(flat_b, cos_table, preferred_element_type=jnp.float32).astype(jnp.bfloat16)
    spec_imag = (-jnp.dot(flat_b, sin_table, preferred_element_type=jnp.float32)).astype(jnp.bfloat16)
    grid_real = jnp.dot(spec_real.T, cos_table, preferred_element_type=jnp.float32) + jnp.dot(spec_imag.T, sin_table, preferred_element_type=jnp.float32)
    grid_imag = jnp.dot(spec_imag.T, cos_table, preferred_element_type=jnp.float32) - jnp.dot(spec_real.T, sin_table, preferred_element_type=jnp.float32)
    return (grid_real, grid_imag)

def adjoint_grid(hold_real, hold_imag, cos_table, sin_table):
    back_real = (jnp.dot(hold_real, cos_table, preferred_element_type=jnp.float32) - jnp.dot(hold_imag, sin_table, preferred_element_type=jnp.float32)).astype(jnp.bfloat16)
    back_imag = (jnp.dot(hold_real, sin_table, preferred_element_type=jnp.float32) + jnp.dot(hold_imag, cos_table, preferred_element_type=jnp.float32)).astype(jnp.bfloat16)
    return jnp.dot(back_real.T, cos_table, preferred_element_type=jnp.float32) - jnp.dot(back_imag.T, sin_table, preferred_element_type=jnp.float32)

def accumulate(positions, values):
    return jnp.zeros((N * N,), jnp.float32).at[positions].add(values)

def reference(image, margin, cells, weights, observed, dual_start):
    highest = lax.Precision.HIGHEST
    cos_table, sin_table = fourier_tables(N)
    column_map = column_matrix(N)
    row_map = row_matrix(ROWS_DEV)
    mask = facet_mask(ROWS_DEV, margin)
    index = jnp.arange(FACETS, dtype=jnp.int32)[:, None] * ROWS_DEV + jnp.arange(ROWS_DEV + 2 * HALO, dtype=jnp.int32)[None, :]
    offsets = jnp.arange(VISIBILITIES, dtype=jnp.int32) // VIS_DEV * (ROWS_DEV * N)
    place = (cells + offsets[None, :]).astype(jnp.int32)
    estimate = image
    lifted = image
    vis_dual = dual_start
    wave_dual = jnp.zeros((CHANNELS, FACETS, ROWS_DEV, N), jnp.float32)
    for iteration in range(ITERS):
        grid_real, grid_imag = lax.map(lambda plane: forward_grid(plane, cos_table, sin_table), lifted)
        model_real = weights * jnp.take_along_axis(grid_real.reshape(CHANNELS, N * N), place, axis=1)
        model_imag = weights * jnp.take_along_axis(grid_imag.reshape(CHANNELS, N * N), place, axis=1)
        model = jnp.stack([model_real, model_imag])
        vis_dual = (vis_dual + (model - observed)) / 2.0
        hold_real = jax.vmap(accumulate)(place, weights * vis_dual[0]).reshape(CHANNELS, N, N).astype(jnp.bfloat16)
        hold_imag = jax.vmap(accumulate)(place, weights * vis_dual[1]).reshape(CHANNELS, N, N).astype(jnp.bfloat16)
        data_term = lax.map(lambda pair: adjoint_grid(pair[0], pair[1], cos_table, sin_table), (hold_real, hold_imag))
        padded = jnp.pad(lifted, ((0, 0), (HALO, HALO), (0, 0)))
        extended = padded[:, index, :] * mask[None, :, :, None]
        filtered = jnp.einsum('cfen,nm->cfem', extended, column_map, precision=highest)
        coef = jnp.einsum('er,cfem->cfrm', row_map, filtered, precision=highest)
        mixed = wave_dual + coef
        total = lax.optimization_barrier(jnp.sum(mixed * mixed, axis=0))
        factor = bound_level / jnp.maximum(jnp.sqrt(total), bound_level)
        wave_dual = mixed * factor[None]
        back = jnp.einsum('cfrm,nm->cfrn', wave_dual, column_map, precision=highest)
        spread = jnp.einsum('er,cfrn->cfen', row_map, back, precision=highest) * mask[None, :, :, None]
        target = jnp.zeros((CHANNELS, N + 2 * HALO, N), jnp.float32).at[:, index, :].add(spread)
        wave_term = target[:, HALO:N + HALO, :]
        fresh = jnp.maximum(estimate - tau_step * (data_term + wave_term), 0.0)
        lifted = 2.0 * fresh - estimate
        estimate = fresh
    return (estimate, vis_dual)
```

```python
import math

import jax
import jax.numpy as jnp
import numpy as np
from jax import lax
from jax.experimental import pallas as pl
from jax.experimental.pallas import tpu as pltpu
from jax.sharding import PartitionSpec as P

N = 1024
ROWS = 32
FACETS = 32
CHANNELS = 16
VIS = 4096
STEP = 512

low_taps = (
    -0.010597401784997278,
    0.032883011666982945,
    0.030841381835986965,
    -0.18703481171888114,
    -0.02798376941698385,
    0.6308807679295904,
    0.7148465705525415,
    0.23037781330885523,
)
high_taps = (
    -0.23037781330885523,
    0.7148465705525415,
    -0.6308807679295904,
    -0.02798376941698385,
    0.18703481171888114,
    0.030841381835986965,
    -0.032883011666982945,
    -0.010597401784997278,
)
tau_step = 0.5
bound_level = 3.0
f32 = jnp.float32
bf16 = jnp.bfloat16


def tap_of(position, line):
    offset = line - position
    if position % 2 == 0:
        return low_taps[offset + 3] if 0 <= offset + 3 < 8 else 0.0
    return high_taps[offset + 4] if 0 <= offset + 4 < 8 else 0.0


def fourier_tables():
    index = np.arange(N, dtype=np.int32)
    product = index[:, None] * index[None, :] % N
    angle = product.astype(np.float32) * np.float32(2.0 * math.pi / N)
    scale = np.float32(1.0 / math.sqrt(N))
    shape = (FACETS, 2, 16, N)
    return (
        (np.cos(angle) * scale).astype(bf16).reshape(shape),
        (np.sin(angle) * scale).astype(bf16).reshape(shape),
    )


def column_weights():
    forward = np.zeros((16, N), np.float32)
    adjoint = np.zeros((16, N), np.float32)
    for shift in range(-4, 5):
        for n in range(N):
            if 0 <= n + shift < N:
                forward[shift + 4, n] = tap_of(n % 2, n % 2 + shift)
                source = n + shift
                adjoint[shift + 4, n] = tap_of(source % 2, source % 2 - shift)
    return forward, adjoint


def row_weights():
    taps = np.zeros((48, 48), np.float32)
    distance = np.zeros((48, 48), np.float32)
    for a in range(40):
        for b in range(48):
            position, line = a - 4, b - 8
            taps[a, b] = tap_of(position, line)
            if position < 0:
                distance[a, b] = max(line + 1, 0)
            elif position < ROWS:
                distance[a, b] = max(-line, line - ROWS + 1, 0)
            else:
                distance[a, b] = max(ROWS - line, 0)
    return taps, distance


def exchange_groups(groups):
    lane = lax.broadcasted_iota(jnp.int32, groups[0].shape, 1)
    g = list(groups)
    for width, pairs in ((64, ((0, 2), (1, 3))), (32, ((0, 1), (2, 3)))):
        first = (lane % (2 * width)) < width
        for a, b in pairs:
            x, y = g[a], g[b]
            g[a] = jnp.where(first, x, pltpu.roll(y, width, 1))
            g[b] = jnp.where(first, pltpu.roll(x, 128 - width, 1), y)
    return g


def pack(real, imag, out_ref):
    for block in range(8):
        span = slice(128 * block, 128 * (block + 1))
        groups = [real[:16, span], real[16:, span], imag[:16, span], imag[16:, span]]
        for d, chunk in enumerate(exchange_groups(groups)):
            out_ref[4 * block + d] = chunk.astype(bf16)


def dot(a, b):
    return jnp.dot(a, b, preferred_element_type=f32)


def forward_kernel(image_ref, cos_ref, sin_ref, out_ref):
    flat = image_ref[0].astype(bf16)
    real = dot(flat, cos_ref[...].reshape(N, N))
    imag = -dot(flat, sin_ref[...].reshape(N, N))
    pack(real, imag, out_ref)


def vis_kernel(
    got_ref, cells_ref, gains_ref, seen_ref, dual_ref, cos_ref, sin_ref, dual_out, out_ref
):
    turned = got_ref[...].reshape(512, 128).T
    by_cos = jnp.zeros((64, N), f32)
    by_sin = jnp.zeros((64, N), f32)
    for h in range(2):
        left = jnp.concatenate(
            [turned[32 * h : 32 * h + 32], turned[64 + 32 * h : 96 + 32 * h]], axis=0
        )
        by_cos = by_cos + dot(left, cos_ref[:, h].reshape(512, N))
        by_sin = by_sin + dot(left, sin_ref[:, h].reshape(512, N))
    grid = (by_cos[:32] + by_sin[32:], by_cos[32:] - by_sin[:32])
    stacked = jnp.concatenate(
        [part[:, 256 * t : 256 * t + 256] for part in grid for t in range(4)], axis=0
    )
    upper = stacked.astype(bf16)
    lower = (stacked - upper.astype(f32)).astype(bf16)
    lines = jnp.concatenate([upper, lower], axis=1)
    cell_lane = lax.broadcasted_iota(jnp.int32, (256, STEP), 0)
    cell_line = lax.broadcasted_iota(jnp.int32, (128, STEP), 0)
    hold = jnp.zeros((256, 256), f32)
    for step in range(VIS // STEP):
        span = slice(STEP * step, STEP * (step + 1))
        cell = cells_ref[:, span]
        lane = cell & 255
        line = ((cell >> 8) & 3) * 32 + (cell >> 10)
        gains = gains_ref[:, span]
        here = jnp.where(cell_lane == lane, 1.0, 0.0).astype(bf16)
        chosen = cell_line == line
        values = dot(lines, jnp.concatenate([here, here], axis=0))
        spread = []
        for c in range(2):
            picked = jnp.sum(
                jnp.where(chosen, values[128 * c : 128 * c + 128], 0.0), axis=0, keepdims=True
            )
            fresh = (dual_ref[c, :, span] + (gains * picked - seen_ref[c, :, span])) / 2.0
            dual_out[c, :, span] = fresh
            spread.append(jnp.where(chosen, gains * fresh, 0.0).astype(bf16))
        hold = hold + lax.dot_general(
            jnp.concatenate(spread, axis=0),
            here,
            (((1,), (1,)), ((), ())),
            preferred_element_type=f32,
        )
    held = hold.astype(bf16)
    held = jnp.concatenate(
        [
            jnp.concatenate(
                [held[128 * c + 32 * t : 128 * c + 32 * t + 32] for t in range(4)], axis=1
            )
            for c in range(2)
        ],
        axis=0,
    )
    by_cos = dot(held, cos_ref[...].reshape(N, N))
    by_sin = dot(held, sin_ref[...].reshape(N, N))
    pack(by_cos[:32] - by_sin[32:], by_sin[:32] + by_cos[32:], out_ref)


def filtered_columns(values, weights_ref):
    total = values * weights_ref[4:5, :]
    for shift in range(-4, 5):
        if shift:
            moved = pltpu.roll(values, (-shift) % N, 1)
            total = total + moved * weights_ref[shift + 4 : shift + 5, :]
    return total


def exact_dot(a, b, dims):
    return lax.dot_general(
        a, b, (dims, ((), ())), precision=lax.Precision.HIGHEST, preferred_element_type=f32
    )


def wave_kernel(
    margin_ref, image_ref, low_ref, high_ref, taps_ref, dist_ref, weights_ref,
    coef_ref, square_ref, rows_ref,
):
    own = margin_ref[0].astype(f32)
    place = lax.broadcasted_iota(jnp.int32, (48, 48), 0)
    above = jnp.broadcast_to(low_ref[0:1, 0:48], (48, 48))
    below = jnp.broadcast_to(high_ref[7:8, 0:48], (48, 48))
    width = jnp.where(place < 4, above, jnp.where(place < 36, own, below))
    rows = jnp.where(dist_ref[...] <= width, taps_ref[...], 0.0)
    rows_ref[...] = rows
    extended = jnp.concatenate([low_ref[...], image_ref[0], high_ref[...]], axis=0)
    coef = filtered_columns(exact_dot(rows, extended, ((1,), (0,))), weights_ref)
    coef_ref[...] = coef
    square = (coef * coef).astype(bf16)
    for block in range(8):
        for half in range(2):
            square_ref[2 * block + half] = square[
                24 * half : 24 * half + 24, 128 * block : 128 * block + 128
            ]


def total_kernel(parts_ref, out_ref):
    total = jnp.sum(parts_ref[...].astype(f32), axis=0).astype(bf16)
    out_ref[...] = jnp.broadcast_to(total[None], out_ref.shape)


def back_kernel(coef_ref, total_ref, rows_ref, weights_ref, out_ref):
    pieces = []
    for half in range(2):
        pieces.append(
            jnp.concatenate(
                [total_ref[2 * block + half].astype(f32) for block in range(8)], axis=1
            )
        )
    total = jnp.concatenate(pieces, axis=0)
    factor = bound_level / jnp.maximum(jnp.sqrt(total), bound_level)
    mixed = exact_dot(rows_ref[...], coef_ref[...] * factor, ((0,), (0,)))
    out_ref[...] = filtered_columns(mixed[8:40], weights_ref)


def final_kernel(got_ref, image_ref, wave_ref, cos_ref, sin_ref, out_ref):
    turned = got_ref[...].reshape(512, 128).T
    total = wave_ref[...]
    for h in range(2):
        total = total + dot(turned[32 * h : 32 * h + 32], cos_ref[:, h].reshape(512, N))
        total = total - dot(turned[64 + 32 * h : 96 + 32 * h], sin_ref[:, h].reshape(512, N))
    out_ref[0] = jnp.maximum(image_ref[0] - tau_step * total, 0.0)


params = pltpu.CompilerParams(vmem_limit_bytes=48 * 1024 * 1024)
in_vmem = pl.BlockSpec(memory_space=pltpu.VMEM)
in_smem = pl.BlockSpec(memory_space=pltpu.SMEM)


def call(kernel, name, out_shape, *args, specs=None):
    return pl.pallas_call(
        kernel,
        out_shape=out_shape,
        in_specs=specs or [in_vmem] * len(args),
        out_specs=jax.tree.map(lambda _: in_vmem, out_shape),
        compiler_params=params,
        name=name,
    )(*args)


def shape(dims, kind):
    return jax.ShapeDtypeStruct(dims, kind)


def local(image, margin, cells, weights, observed, dual_start):
    cos_table, sin_table = (jnp.asarray(t) for t in fourier_tables())
    forward_weights, adjoint_weights = (jnp.asarray(t) for t in column_weights())
    taps, distance = (jnp.asarray(t) for t in row_weights())
    chunks = shape((FACETS, 16, 128), bf16)
    squares = shape((CHANNELS, 24, 128), bf16)
    wide = jnp.broadcast_to(margin.astype(f32)[:, None], (1, N))
    up = [(i, i + 1) for i in range(FACETS - 1)]
    down = [(i + 1, i) for i in range(FACETS - 1)]
    low = lax.ppermute(jnp.concatenate([wide, image[0, 25:]], axis=0), "slab", up)
    high = lax.ppermute(jnp.concatenate([image[0, :7], wide], axis=0), "slab", down)
    sent = call(forward_kernel, "rows_out", chunks, image, cos_table, sin_table)
    got = lax.all_to_all(sent, "slab", 0, 0, tiled=True)
    coef, square, rows = call(
        wave_kernel,
        "wave_out",
        (shape((48, N), f32), squares, shape((48, 48), f32)),
        margin, image, low, high, taps, distance, forward_weights,
        specs=[in_smem] + [in_vmem] * 6,
    )
    parts = lax.all_to_all(square, "chan", 0, 0, tiled=True)
    copies = call(total_kernel, "wave_sum", squares, parts)
    totals = lax.all_to_all(copies, "chan", 0, 0, tiled=True)
    wave = call(
        back_kernel, "wave_back", shape((ROWS, N), f32), coef, totals, rows, adjoint_weights
    )
    dual, back = call(
        vis_kernel,
        "visibilities",
        (shape((2, 1, VIS), f32), chunks),
        got, cells, weights, observed, dual_start, cos_table, sin_table,
    )
    returned = lax.all_to_all(back, "slab", 0, 0, tiled=True)
    fresh = call(
        final_kernel, "image_out", shape((1, ROWS, N), f32),
        returned, image, wave, cos_table, sin_table,
    )
    return (fresh, dual)


def solution(mesh):
    in_specs = (
        P("chan", "slab", None),
        P("slab"),
        P("chan", "slab"),
        P("chan", "slab"),
        P(None, "chan", "slab"),
        P(None, "chan", "slab"),
    )
    out_specs = (P("chan", "slab", None), P(None, "chan", "slab"))
    return jax.shard_map(local, mesh=mesh, in_specs=in_specs, out_specs=out_specs, check_vma=False)
```

```python
import math

import jax
import jax.numpy as jnp
import numpy as np
from jax import lax
from jax.experimental import pallas as pl
from jax.experimental.pallas import tpu as pltpu
from jax.sharding import PartitionSpec as P

N = 1024
HALF = 512
ROWS = 32
FACETS = 32
CHANNELS = 16
VIS = 4096
STEP = 512

low_taps = (
    -0.010597401784997278,
    0.032883011666982945,
    0.030841381835986965,
    -0.18703481171888114,
    -0.02798376941698385,
    0.6308807679295904,
    0.7148465705525415,
    0.23037781330885523,
)
high_taps = (
    -0.23037781330885523,
    0.7148465705525415,
    -0.6308807679295904,
    -0.02798376941698385,
    0.18703481171888114,
    0.030841381835986965,
    -0.032883011666982945,
    -0.010597401784997278,
)
tau_step = 0.5
bound_level = 3.0
f32 = jnp.float32
bf16 = jnp.bfloat16


def fourier_tables():
    index = np.arange(HALF, dtype=np.int32)
    product = index[:, None] * index[None, :] % N
    angle = product.astype(np.float32) * np.float32(2.0 * math.pi / N)
    scale = np.float32(1.0 / math.sqrt(N))
    shape = (FACETS // 2, 2, 16, HALF)
    return (
        (np.cos(angle) * scale).astype(bf16).reshape(shape),
        (np.sin(angle) * scale).astype(bf16).reshape(shape),
    )


def tap_pair(shift):
    even = low_taps[shift + 3] if 0 <= shift + 3 < 8 else 0.0
    odd = high_taps[shift + 4] if 0 <= shift + 4 < 8 else 0.0
    return even, odd


def row_weights(above, own, below):
    place = lax.broadcasted_iota(jnp.int32, (48, 48), 0)
    position = place - 4
    line = lax.broadcasted_iota(jnp.int32, (48, 48), 1) - 8
    even = position % 2 == 0
    taps = jnp.zeros((48, 48), f32)
    for shift in range(-4, 5):
        pair = tap_pair(shift)
        taps = jnp.where(line - position == shift, jnp.where(even, *pair), taps)
    inside = jnp.maximum(jnp.maximum(-line, line - ROWS + 1), 0)
    distance = jnp.where(
        place < 4,
        jnp.maximum(line + 1, 0),
        jnp.where(place < 36, inside, jnp.maximum(ROWS - line, 0)),
    )
    width = jnp.where(place < 4, above, jnp.where(place < 36, own, below))
    return jnp.where((distance.astype(f32) <= width) & (place < 40), taps, 0.0)


def exchange_groups(groups):
    lane = lax.broadcasted_iota(jnp.int32, groups[0].shape, 1)
    g = list(groups)
    for width, pairs in ((64, ((0, 2), (1, 3))), (32, ((0, 1), (2, 3)))):
        first = (lane % (2 * width)) < width
        for a, b in pairs:
            x, y = g[a], g[b]
            g[a] = jnp.where(first, x, pltpu.roll(y, width, 1))
            g[b] = jnp.where(first, pltpu.roll(x, 128 - width, 1), y)
    return g


def pack(real, imag, out_ref):
    for block in range(8):
        span = slice(128 * block, 128 * (block + 1))
        groups = [real[:16, span], real[16:, span], imag[:16, span], imag[16:, span]]
        for d, chunk in enumerate(exchange_groups(groups)):
            out_ref[4 * block + d] = chunk.astype(bf16)


def dot(a, b):
    return jnp.dot(a, b, preferred_element_type=f32)


def signs(dims):
    return jnp.where(lax.broadcasted_iota(jnp.int32, dims, 1) % 2 == 0, 1.0, -1.0)


def quarters(low, high):
    sign = signs(low.shape).astype(bf16)
    return jnp.concatenate([low, high, low * sign, high * sign], axis=0)


def whole(products):
    rows = products.shape[0] // 4
    sign = signs((rows, HALF))
    part = [products[rows * t : rows * t + rows] for t in range(4)]
    return jnp.concatenate([part[0] + sign * part[1], part[2] + sign * part[3]], axis=1)


def regrouped(table_ref):
    return jnp.concatenate([table_ref[:, h].reshape(256, HALF) for h in range(2)], axis=0)


def split(pieces):
    return (
        jnp.concatenate([p[:, :256] for p in pieces], axis=1),
        jnp.concatenate([p[:, 256:] for p in pieces], axis=1),
    )


def forward_kernel(
    margin_ref, image_ref, cos_ref, sin_ref,
    out_ref, low_ref, high_ref, held_ref, cos_out, sin_out, image_sem, table_sems,
):
    image_copy = pltpu.make_async_copy(image_ref.at[0], held_ref, image_sem)
    image_copy.start()
    copies = [
        pltpu.make_async_copy(cos_ref, cos_out, table_sems.at[0]),
        pltpu.make_async_copy(sin_ref, sin_out, table_sems.at[1]),
    ]
    for copy in copies:
        copy.start()
    image_copy.wait()
    width = jnp.broadcast_to(margin_ref[0].astype(f32), (8, N))
    line = lax.broadcasted_iota(jnp.int32, (8, N), 0)
    low_ref[...] = jnp.where(line == 0, width, held_ref[24:, :])
    high_ref[...] = jnp.where(line == 7, width, held_ref[:8, :])
    flat = held_ref[...].astype(bf16)
    left = quarters(flat[:, :HALF], flat[:, HALF:])
    copies[0].wait()
    real = whole(dot(left, cos_out[...].reshape(HALF, HALF)))
    copies[1].wait()
    imag = -whole(dot(left, sin_out[...].reshape(HALF, HALF)))
    pack(real, imag, out_ref)


def vis_kernel(
    got_ref, cells_ref, gains_ref, seen_ref, dual_ref, cos_ref, sin_ref, dual_out, out_ref
):
    turned = got_ref[...].reshape(512, 128).T
    left = quarters(
        *split(
            [
                jnp.concatenate(
                    [turned[32 * h : 32 * h + 32], turned[64 + 32 * h : 96 + 32 * h]], axis=0
                )
                for h in range(2)
            ]
        )
    )
    by_cos = whole(dot(left, regrouped(cos_ref)))
    by_sin = whole(dot(left, regrouped(sin_ref)))
    grid = (by_cos[:32] + by_sin[32:], by_cos[32:] - by_sin[:32])
    stacked = jnp.concatenate(
        [part[:, 256 * t : 256 * t + 256] for part in grid for t in range(4)], axis=0
    )
    upper = stacked.astype(bf16)
    lower = (stacked - upper.astype(f32)).astype(bf16)
    lines = jnp.concatenate([upper, lower], axis=1)
    cell_lane = lax.broadcasted_iota(jnp.int32, (256, STEP), 0)
    cell_line = lax.broadcasted_iota(jnp.int32, (128, STEP), 0)
    hold = jnp.zeros((256, 256), f32)
    for step in range(VIS // STEP):
        span = slice(STEP * step, STEP * (step + 1))
        cell = cells_ref[:, span]
        lane = cell & 255
        line = ((cell >> 8) & 3) * 32 + (cell >> 10)
        gains = gains_ref[:, span]
        here = jnp.where(cell_lane == lane, 1.0, 0.0).astype(bf16)
        chosen = cell_line == line
        values = dot(lines, jnp.concatenate([here, here], axis=0))
        spread = []
        for c in range(2):
            picked = jnp.sum(
                jnp.where(chosen, values[128 * c : 128 * c + 128], 0.0), axis=0, keepdims=True
            )
            fresh = (dual_ref[c, :, span] + (gains * picked - seen_ref[c, :, span])) / 2.0
            dual_out[c, :, span] = fresh
            spread.append(jnp.where(chosen, gains * fresh, 0.0).astype(bf16))
        hold = hold + lax.dot_general(
            jnp.concatenate(spread, axis=0),
            here,
            (((1,), (1,)), ((), ())),
            preferred_element_type=f32,
        )
    held = hold.astype(bf16)
    held = jnp.concatenate(
        [
            jnp.concatenate(
                [held[128 * c + 32 * t : 128 * c + 32 * t + 32] for t in range(4)], axis=1
            )
            for c in range(2)
        ],
        axis=0,
    )
    left = quarters(held[:, :HALF], held[:, HALF:])
    by_cos = whole(dot(left, cos_ref[...].reshape(HALF, HALF)))
    by_sin = whole(dot(left, sin_ref[...].reshape(HALF, HALF)))
    pack(by_cos[:32] - by_sin[32:], by_sin[:32] + by_cos[32:], out_ref)


def filtered_columns(values, adjoint):
    rows = values.shape[0]
    padded = jnp.concatenate([values, jnp.zeros((rows, 128), f32)], axis=1)
    even = lax.broadcasted_iota(jnp.int32, (rows, N), 1) % 2 == 0
    total = jnp.zeros((rows, N), f32)
    for shift in range(-4, 5):
        moved = pltpu.roll(padded, (-shift) % (N + 128), 1)[:, :N] if shift else values
        pair = tap_pair(-shift if adjoint else shift)
        if adjoint and shift % 2:
            pair = pair[::-1]
        total = total + moved * jnp.where(even, *pair)
    return total


def exact_dot(a, b, dims):
    return lax.dot_general(
        a, b, (dims, ((), ())), precision=lax.Precision.HIGHEST, preferred_element_type=f32
    )


def wave_kernel(
    margin_ref, image_ref, low_ref, high_ref, coef_ref, square_ref, rows_ref
):
    above = jnp.broadcast_to(low_ref[0:1, 0:48], (48, 48))
    below = jnp.broadcast_to(high_ref[7:8, 0:48], (48, 48))
    rows = row_weights(above, margin_ref[0].astype(f32), below)
    rows_ref[...] = rows
    extended = jnp.concatenate([low_ref[...], image_ref[...], high_ref[...]], axis=0)
    coef = filtered_columns(exact_dot(rows, extended, ((1,), (0,))), False)
    coef_ref[...] = coef
    square_ref[...] = (coef * coef)[:40].astype(bf16)


def back_kernel(coef_ref, rows_ref, *refs):
    total = sum(ref[...].astype(f32) for ref in refs[:-1])
    factor = bound_level / jnp.maximum(jnp.sqrt(total), bound_level)
    mixed = exact_dot(rows_ref[0:40, :], coef_ref[0:40, :] * factor, ((0,), (0,)))
    refs[-1][...] = filtered_columns(mixed[8:40], True)


def join_kernel(*refs):
    refs[-1][...] = sum(ref[...].astype(f32) for ref in refs[:-1]).astype(bf16)


def final_kernel(got_ref, image_ref, wave_ref, cos_ref, sin_ref, out_ref):
    turned = got_ref[...].reshape(512, 128).T
    real = quarters(*split([turned[:32], turned[32:64]]))
    imag = quarters(*split([turned[64:96], turned[96:]]))
    data = whole(dot(real, regrouped(cos_ref)) - dot(imag, regrouped(sin_ref)))
    total = data + wave_ref[...]
    out_ref[0] = jnp.maximum(image_ref[...] - tau_step * total, 0.0)


in_vmem = pl.BlockSpec(memory_space=pltpu.VMEM)
in_smem = pl.BlockSpec(memory_space=pltpu.SMEM)
in_hbm = pl.BlockSpec(memory_space=pltpu.HBM)


def call(kernel, name, out_shape, *args, specs=None, scratch=(), room=12):
    return pl.pallas_call(
        kernel,
        out_shape=out_shape,
        in_specs=specs or [in_vmem] * len(args),
        out_specs=jax.tree.map(lambda _: in_vmem, out_shape),
        scratch_shapes=list(scratch),
        compiler_params=pltpu.CompilerParams(vmem_limit_bytes=room * 1024 * 1024),
        name=name,
    )(*args)


def shape(dims, kind):
    return jax.ShapeDtypeStruct(dims, kind)


def swapped(value, steps):
    moved = [lax.ppermute(value, "chan", [(i, i ^ s) for i in range(CHANNELS)]) for s in steps]
    return [value] + moved


def local(image, margin, cells, weights, observed, dual_start):
    cos_table, sin_table = (jnp.asarray(t) for t in fourier_tables())
    chunks = shape((FACETS, 16, 128), bf16)
    squares = shape((40, N), bf16)
    edge = shape((8, N), f32)
    table = shape(cos_table.shape, bf16)
    up = [(i, i + 1) for i in range(FACETS - 1)]
    down = [(i + 1, i) for i in range(FACETS - 1)]
    sent, low, high, held, cos_held, sin_held = call(
        forward_kernel,
        "rows_out",
        (chunks, edge, edge, shape((ROWS, N), f32), table, table),
        margin, image, cos_table, sin_table,
        specs=[in_smem] + [in_hbm] * 3,
        scratch=[pltpu.SemaphoreType.DMA, pltpu.SemaphoreType.DMA((2,))],
    )
    got = lax.all_to_all(sent, "slab", 0, 0, tiled=True)
    low = lax.ppermute(low, "slab", up)
    high = lax.ppermute(high, "slab", down)
    coef, square, rows = call(
        wave_kernel,
        "wave_out",
        (shape((48, N), f32), squares, shape((48, 48), f32)),
        margin, held, low, high,
        specs=[in_smem] + [in_vmem] * 3,
    )
    part = call(join_kernel, "wave_part", squares, *swapped(square, (1, 8, 9)))
    got, part = lax.optimization_barrier((got, part))
    dual, back = call(
        vis_kernel,
        "visibilities",
        (shape((2, 1, VIS), f32), chunks),
        got, cells, weights, observed, dual_start, cos_held, sin_held,
    )
    returned = lax.all_to_all(back, "slab", 0, 0, tiled=True)
    wave = call(
        back_kernel, "wave_back", shape((ROWS, N), f32), coef, rows, *swapped(part, (2, 4, 6))
    )
    fresh = call(
        final_kernel, "image_out", shape((1, ROWS, N), f32),
        returned, held, wave, cos_held, sin_held,
    )
    return (fresh, dual)


def solution(mesh):
    in_specs = (
        P("chan", "slab", None),
        P("slab"),
        P("chan", "slab"),
        P("chan", "slab"),
        P(None, "chan", "slab"),
        P(None, "chan", "slab"),
    )
    out_specs = (P("chan", "slab", None), P(None, "chan", "slab"))
    return jax.shard_map(local, mesh=mesh, in_specs=in_specs, out_specs=out_specs, check_vma=False)
```

```python
import math

import jax
import jax.numpy as jnp
import numpy as np
from jax import lax
from jax.experimental import pallas as pl
from jax.experimental.pallas import tpu as pltpu
from jax.sharding import PartitionSpec as P

N = 1024
HALF = 512
ROWS = 32
FACETS = 32
CHANNELS = 16
VIS = 4096
STEP = 512

low_taps = (
    -0.010597401784997278,
    0.032883011666982945,
    0.030841381835986965,
    -0.18703481171888114,
    -0.02798376941698385,
    0.6308807679295904,
    0.7148465705525415,
    0.23037781330885523,
)
high_taps = (
    -0.23037781330885523,
    0.7148465705525415,
    -0.6308807679295904,
    -0.02798376941698385,
    0.18703481171888114,
    0.030841381835986965,
    -0.032883011666982945,
    -0.010597401784997278,
)
tau_step = 0.5
bound_level = 3.0
f32 = jnp.float32
bf16 = jnp.bfloat16


def fourier_tables():
    index = np.arange(HALF, dtype=np.int32)
    product = index[:, None] * index[None, :] % N
    angle = product.astype(np.float32) * np.float32(2.0 * math.pi / N)
    scale = np.float32(1.0 / math.sqrt(N))
    shape = (2, FACETS // 2, 2, 16, HALF)
    pair = np.stack([np.cos(angle) * scale, np.sin(angle) * scale])
    return pair.astype(bf16).reshape(shape)


def tap_pair(shift):
    even = low_taps[shift + 3] if 0 <= shift + 3 < 8 else 0.0
    odd = high_taps[shift + 4] if 0 <= shift + 4 < 8 else 0.0
    return even, odd


def row_weights(above, own, below):
    place = lax.broadcasted_iota(jnp.int32, (48, 48), 0)
    position = place - 4
    line = lax.broadcasted_iota(jnp.int32, (48, 48), 1) - 8
    even = position % 2 == 0
    taps = jnp.zeros((48, 48), f32)
    for shift in range(-4, 5):
        pair = tap_pair(shift)
        taps = jnp.where(line - position == shift, jnp.where(even, *pair), taps)
    inside = jnp.maximum(jnp.maximum(-line, line - ROWS + 1), 0)
    distance = jnp.where(
        place < 4,
        jnp.maximum(line + 1, 0),
        jnp.where(place < 36, inside, jnp.maximum(ROWS - line, 0)),
    )
    width = jnp.where(place < 4, above, jnp.where(place < 36, own, below))
    return jnp.where((distance.astype(f32) <= width) & (place < 40), taps, 0.0)


def exchange_groups(groups):
    lane = lax.broadcasted_iota(jnp.int32, groups[0].shape, 1)
    g = list(groups)
    for width, pairs in ((64, ((0, 2), (1, 3))), (32, ((0, 1), (2, 3)))):
        first = (lane % (2 * width)) < width
        for a, b in pairs:
            x, y = g[a], g[b]
            g[a] = jnp.where(first, x, pltpu.roll(y, width, 1))
            g[b] = jnp.where(first, pltpu.roll(x, 128 - width, 1), y)
    return g


def pack(real, imag, out_ref):
    for block in range(8):
        span = slice(128 * block, 128 * (block + 1))
        groups = [real[:16, span], real[16:, span], imag[:16, span], imag[16:, span]]
        for d, chunk in enumerate(exchange_groups(groups)):
            out_ref[4 * block + d] = chunk.astype(bf16)


def dot(a, b):
    return jnp.dot(a, b, preferred_element_type=f32)


def signs(dims):
    return jnp.where(lax.broadcasted_iota(jnp.int32, dims, 1) % 2 == 0, 1.0, -1.0)


def quarters(low, high):
    sign = signs(low.shape).astype(bf16)
    return jnp.concatenate([low, high, low * sign, high * sign], axis=0)


def whole(products):
    rows = products.shape[0] // 4
    sign = signs((rows, HALF))
    part = [products[rows * t : rows * t + rows] for t in range(4)]
    return jnp.concatenate([part[0] + sign * part[1], part[2] + sign * part[3]], axis=1)


def plain(tables_ref, which):
    return tables_ref[which].reshape(HALF, HALF)


def regrouped(tables_ref, which):
    parts = [tables_ref[which, :, h].reshape(256, HALF) for h in range(2)]
    return jnp.concatenate(parts, axis=0)


def split(pieces):
    return (
        jnp.concatenate([p[:, :256] for p in pieces], axis=1),
        jnp.concatenate([p[:, 256:] for p in pieces], axis=1),
    )


def forward_kernel(image_ref, tables_ref, out_ref, held_ref, tables_out, image_sem, table_sem):
    image_copy = pltpu.make_async_copy(image_ref.at[0], held_ref, image_sem)
    tables_copy = pltpu.make_async_copy(tables_ref, tables_out, table_sem)
    image_copy.start()
    tables_copy.start()
    image_copy.wait()
    flat = held_ref[...].astype(bf16)
    left = quarters(flat[:, :HALF], flat[:, HALF:])
    tables_copy.wait()
    pack(whole(dot(left, plain(tables_out, 0))), -whole(dot(left, plain(tables_out, 1))), out_ref)


def vis_kernel(
    got_ref, cells_ref, gains_ref, seen_ref, dual_ref, tables_ref, dual_out, out_ref
):
    turned = got_ref[...].reshape(512, 128).T
    left = quarters(
        *split(
            [
                jnp.concatenate(
                    [turned[32 * h : 32 * h + 32], turned[64 + 32 * h : 96 + 32 * h]], axis=0
                )
                for h in range(2)
            ]
        )
    )
    by_cos = whole(dot(left, regrouped(tables_ref, 0)))
    by_sin = whole(dot(left, regrouped(tables_ref, 1)))
    grid = (by_cos[:32] + by_sin[32:], by_cos[32:] - by_sin[:32])
    stacked = jnp.concatenate(
        [part[:, 256 * t : 256 * t + 256] for part in grid for t in range(4)], axis=0
    )
    upper = stacked.astype(bf16)
    lower = (stacked - upper.astype(f32)).astype(bf16)
    lines = jnp.concatenate([upper, lower], axis=1)
    cell_lane = lax.broadcasted_iota(jnp.int32, (256, STEP), 0)
    cell_line = lax.broadcasted_iota(jnp.int32, (128, STEP), 0)
    hold = jnp.zeros((256, 256), f32)
    for step in range(VIS // STEP):
        span = slice(STEP * step, STEP * (step + 1))
        cell = cells_ref[:, span]
        lane = cell & 255
        line = ((cell >> 8) & 3) * 32 + (cell >> 10)
        gains = gains_ref[:, span]
        here = jnp.where(cell_lane == lane, 1.0, 0.0).astype(bf16)
        chosen = cell_line == line
        values = dot(lines, jnp.concatenate([here, here], axis=0))
        spread = []
        for c in range(2):
            picked = jnp.sum(
                jnp.where(chosen, values[128 * c : 128 * c + 128], 0.0), axis=0, keepdims=True
            )
            fresh = (dual_ref[c, :, span] + (gains * picked - seen_ref[c, :, span])) / 2.0
            dual_out[c, :, span] = fresh
            spread.append(jnp.where(chosen, gains * fresh, 0.0).astype(bf16))
        hold = hold + lax.dot_general(
            jnp.concatenate(spread, axis=0),
            here,
            (((1,), (1,)), ((), ())),
            preferred_element_type=f32,
        )
    held = hold.astype(bf16)
    held = jnp.concatenate(
        [
            jnp.concatenate(
                [held[128 * c + 32 * t : 128 * c + 32 * t + 32] for t in range(4)], axis=1
            )
            for c in range(2)
        ],
        axis=0,
    )
    left = quarters(held[:, :HALF], held[:, HALF:])
    by_cos = whole(dot(left, plain(tables_ref, 0)))
    by_sin = whole(dot(left, plain(tables_ref, 1)))
    pack(by_cos[:32] - by_sin[32:], by_sin[:32] + by_cos[32:], out_ref)


def filtered_columns(values, adjoint):
    rows = values.shape[0]
    padded = jnp.concatenate([values, jnp.zeros((rows, 128), f32)], axis=1)
    even = lax.broadcasted_iota(jnp.int32, (rows, N), 1) % 2 == 0
    total = jnp.zeros((rows, N), f32)
    for shift in range(-4, 5):
        moved = pltpu.roll(padded, (-shift) % (N + 128), 1)[:, :N] if shift else values
        pair = tap_pair(-shift if adjoint else shift)
        if adjoint and shift % 2:
            pair = pair[::-1]
        total = total + moved * jnp.where(even, *pair)
    return total


def exact_dot(a, b, dims):
    return lax.dot_general(
        a, b, (dims, ((), ())), precision=lax.Precision.HIGHEST, preferred_element_type=f32
    )


def wave_kernel(
    margin_ref, image_ref, low_ref, high_ref, coef_ref, square_ref, rows_ref
):
    above = jnp.broadcast_to(low_ref[0:1, 0:48], (48, 48))
    below = jnp.broadcast_to(high_ref[7:8, 0:48], (48, 48))
    rows = row_weights(above, margin_ref[0].astype(f32), below)
    rows_ref[...] = rows
    extended = jnp.concatenate([low_ref[...], image_ref[...], high_ref[...]], axis=0)
    coef = filtered_columns(exact_dot(rows, extended, ((1,), (0,))), False)
    coef_ref[...] = coef
    square_ref[...] = (coef * coef)[:40].astype(bf16)


def join_kernel(parts_ref, out_ref):
    out_ref[...] = jnp.sum(parts_ref[...].astype(f32), axis=0).astype(bf16)


def back_kernel(coef_ref, rows_ref, parts_ref, out_ref):
    total = jnp.sum(parts_ref[...].astype(f32), axis=0)
    factor = bound_level / jnp.maximum(jnp.sqrt(total), bound_level)
    mixed = exact_dot(rows_ref[0:40, :], coef_ref[0:40, :] * factor, ((0,), (0,)))
    out_ref[...] = filtered_columns(mixed[8:40], True)


def final_kernel(got_ref, image_ref, wave_ref, tables_ref, out_ref):
    turned = got_ref[...].reshape(512, 128).T
    real = quarters(*split([turned[:32], turned[32:64]]))
    imag = quarters(*split([turned[64:96], turned[96:]]))
    data = whole(dot(real, regrouped(tables_ref, 0)) - dot(imag, regrouped(tables_ref, 1)))
    total = data + wave_ref[...]
    out_ref[0] = jnp.maximum(image_ref[...] - tau_step * total, 0.0)


in_vmem = pl.BlockSpec(memory_space=pltpu.VMEM)
in_smem = pl.BlockSpec(memory_space=pltpu.SMEM)
in_hbm = pl.BlockSpec(memory_space=pltpu.HBM)


def call(kernel, name, out_shape, *args, specs=None, scratch=(), room=12):
    return pl.pallas_call(
        kernel,
        out_shape=out_shape,
        in_specs=specs or [in_vmem] * len(args),
        out_specs=jax.tree.map(lambda _: in_vmem, out_shape),
        scratch_shapes=list(scratch),
        compiler_params=pltpu.CompilerParams(vmem_limit_bytes=room * 1024 * 1024),
        name=name,
    )(*args)


def shape(dims, kind):
    return jax.ShapeDtypeStruct(dims, kind)


def local(image, margin, cells, weights, observed, dual_start):
    tables = jnp.asarray(fourier_tables())
    chunks = shape((FACETS, 16, 128), bf16)
    squares = shape((40, N), bf16)
    up = [(i, i + 1) for i in range(FACETS - 1)]
    down = [(i + 1, i) for i in range(FACETS - 1)]
    wide = jnp.broadcast_to(margin.astype(f32)[:, None], (1, N))
    low = lax.ppermute(jnp.concatenate([wide, image[0, 25:]], axis=0), "slab", up)
    high = lax.ppermute(jnp.concatenate([image[0, :7], wide], axis=0), "slab", down)
    sent, held, tables_held = call(
        forward_kernel,
        "rows_out",
        (chunks, shape((ROWS, N), f32), shape(tables.shape, bf16)),
        image, tables,
        specs=[in_hbm] * 2,
        scratch=[pltpu.SemaphoreType.DMA, pltpu.SemaphoreType.DMA],
    )
    sent, low, high = lax.optimization_barrier((sent, low, high))
    coef, square, rows = call(
        wave_kernel,
        "wave_out",
        (shape((48, N), f32), squares, shape((48, 48), f32)),
        margin, held, low, high,
        specs=[in_smem] + [in_vmem] * 3,
    )
    got = lax.all_to_all(sent, "slab", 0, 0, tiled=True)
    near = [[c, c + 1, c + 8, c + 9] for c in (0, 2, 4, 6)]
    far = [[c, c + 2, c + 4, c + 6] for c in (0, 1, 8, 9)]
    parts = lax.all_gather(square, "chan", axis_index_groups=near)
    part = call(join_kernel, "wave_part", squares, parts)
    got, part = lax.optimization_barrier((got, part))
    dual, back = call(
        vis_kernel,
        "visibilities",
        (shape((2, 1, VIS), f32), chunks),
        got, cells, weights, observed, dual_start, tables_held,
    )
    returned = lax.all_to_all(back, "slab", 0, 0, tiled=True)
    gathered = lax.all_gather(part, "chan", axis_index_groups=far)
    wave = call(back_kernel, "wave_back", shape((ROWS, N), f32), coef, rows, gathered)
    fresh = call(
        final_kernel, "image_out", shape((1, ROWS, N), f32),
        returned, held, wave, tables_held,
    )
    return (fresh, dual)


def solution(mesh):
    in_specs = (
        P("chan", "slab", None),
        P("slab"),
        P("chan", "slab"),
        P("chan", "slab"),
        P(None, "chan", "slab"),
        P(None, "chan", "slab"),
    )
    out_specs = (P("chan", "slab", None), P(None, "chan", "slab"))
    return jax.shard_map(local, mesh=mesh, in_specs=in_specs, out_specs=out_specs, check_vma=False)
```

```python
import math

import jax
import jax.numpy as jnp
import numpy as np
from jax import lax
from jax.experimental import pallas as pl
from jax.experimental.pallas import tpu as pltpu
from jax.sharding import PartitionSpec as P

N = 1024
HALF = 512
ROWS = 32
FACETS = 32
CHANNELS = 16
VIS = 4096
STEP = 512

low_taps = (
    -0.010597401784997278,
    0.032883011666982945,
    0.030841381835986965,
    -0.18703481171888114,
    -0.02798376941698385,
    0.6308807679295904,
    0.7148465705525415,
    0.23037781330885523,
)
high_taps = (
    -0.23037781330885523,
    0.7148465705525415,
    -0.6308807679295904,
    -0.02798376941698385,
    0.18703481171888114,
    0.030841381835986965,
    -0.032883011666982945,
    -0.010597401784997278,
)
tau_step = 0.5
bound_level = 3.0
f32 = jnp.float32
bf16 = jnp.bfloat16


def fourier_tables():
    index = np.arange(HALF, dtype=np.int32)
    product = index[:, None] * index[None, :] % N
    angle = product.astype(np.float32) * np.float32(2.0 * math.pi / N)
    scale = np.float32(1.0 / math.sqrt(N))
    shape = (2, FACETS // 2, 2, 16, HALF)
    pair = np.stack([np.cos(angle) * scale, np.sin(angle) * scale])
    return pair.astype(bf16).reshape(shape)


def tap_pair(shift):
    even = low_taps[shift + 3] if 0 <= shift + 3 < 8 else 0.0
    odd = high_taps[shift + 4] if 0 <= shift + 4 < 8 else 0.0
    return even, odd


def row_weights(above, own, below):
    place = lax.broadcasted_iota(jnp.int32, (48, 48), 0)
    position = place - 4
    line = lax.broadcasted_iota(jnp.int32, (48, 48), 1) - 8
    even = position % 2 == 0
    taps = jnp.zeros((48, 48), f32)
    for shift in range(-4, 5):
        pair = tap_pair(shift)
        taps = jnp.where(line - position == shift, jnp.where(even, *pair), taps)
    inside = jnp.maximum(jnp.maximum(-line, line - ROWS + 1), 0)
    distance = jnp.where(
        place < 4,
        jnp.maximum(line + 1, 0),
        jnp.where(place < 36, inside, jnp.maximum(ROWS - line, 0)),
    )
    width = jnp.where(place < 4, above, jnp.where(place < 36, own, below))
    return jnp.where((distance.astype(f32) <= width) & (place < 40), taps, 0.0)


def exchange_groups(groups):
    lane = lax.broadcasted_iota(jnp.int32, groups[0].shape, 1)
    g = list(groups)
    for width, pairs in ((64, ((0, 2), (1, 3))), (32, ((0, 1), (2, 3)))):
        first = (lane % (2 * width)) < width
        for a, b in pairs:
            x, y = g[a], g[b]
            g[a] = jnp.where(first, x, pltpu.roll(y, width, 1))
            g[b] = jnp.where(first, pltpu.roll(x, 128 - width, 1), y)
    return g


def pack(real, imag, out_ref):
    for block in range(8):
        span = slice(128 * block, 128 * (block + 1))
        groups = [real[:16, span], real[16:, span], imag[:16, span], imag[16:, span]]
        for d, chunk in enumerate(exchange_groups(groups)):
            out_ref[4 * block + d] = chunk.astype(bf16)


def dot(a, b):
    return jnp.dot(a, b, preferred_element_type=f32)


def signs(dims):
    return jnp.where(lax.broadcasted_iota(jnp.int32, dims, 1) % 2 == 0, 1.0, -1.0)


def quarters(low, high):
    sign = signs(low.shape).astype(bf16)
    return jnp.concatenate([low, high, low * sign, high * sign], axis=0)


def whole(products):
    rows = products.shape[0] // 4
    sign = signs((rows, HALF))
    part = [products[rows * t : rows * t + rows] for t in range(4)]
    return jnp.concatenate([part[0] + sign * part[1], part[2] + sign * part[3]], axis=1)


def plain(tables_ref, which):
    return tables_ref[which].reshape(HALF, HALF)


def regrouped(tables_ref, which):
    parts = [tables_ref[which, :, h].reshape(256, HALF) for h in range(2)]
    return jnp.concatenate(parts, axis=0)


def split(pieces):
    return (
        jnp.concatenate([p[:, :256] for p in pieces], axis=1),
        jnp.concatenate([p[:, 256:] for p in pieces], axis=1),
    )


def forward_kernel(image_ref, tables_ref, out_ref, held_ref, tables_out, image_sem, table_sem):
    image_copy = pltpu.make_async_copy(image_ref.at[0], held_ref, image_sem)
    tables_copy = pltpu.make_async_copy(tables_ref, tables_out, table_sem)
    image_copy.start()
    tables_copy.start()
    image_copy.wait()
    flat = held_ref[...].astype(bf16)
    left = quarters(flat[:, :HALF], flat[:, HALF:])
    tables_copy.wait()
    pack(whole(dot(left, plain(tables_out, 0))), -whole(dot(left, plain(tables_out, 1))), out_ref)


def vis_kernel(
    got_ref, cells_ref, gains_ref, seen_ref, dual_ref, tables_ref, dual_out, out_ref
):
    turned = got_ref[...].reshape(512, 128).T
    left = quarters(
        *split(
            [
                jnp.concatenate(
                    [turned[32 * h : 32 * h + 32], turned[64 + 32 * h : 96 + 32 * h]], axis=0
                )
                for h in range(2)
            ]
        )
    )
    by_cos = whole(dot(left, regrouped(tables_ref, 0)))
    by_sin = whole(dot(left, regrouped(tables_ref, 1)))
    grid = (by_cos[:32] + by_sin[32:], by_cos[32:] - by_sin[:32])
    stacked = jnp.concatenate(
        [part[:, 256 * t : 256 * t + 256] for part in grid for t in range(4)], axis=0
    )
    upper = stacked.astype(bf16)
    lower = (stacked - upper.astype(f32)).astype(bf16)
    lines = jnp.concatenate([upper, lower], axis=1)
    cell_lane = lax.broadcasted_iota(jnp.int32, (256, STEP), 0)
    cell_line = lax.broadcasted_iota(jnp.int32, (128, STEP), 0)
    hold = jnp.zeros((256, 256), f32)
    for step in range(VIS // STEP):
        span = slice(STEP * step, STEP * (step + 1))
        cell = cells_ref[:, span]
        lane = cell & 255
        line = ((cell >> 8) & 3) * 32 + (cell >> 10)
        gains = gains_ref[:, span]
        here = jnp.where(cell_lane == lane, 1.0, 0.0).astype(bf16)
        chosen = cell_line == line
        values = dot(lines, jnp.concatenate([here, here], axis=0))
        spread = []
        for c in range(2):
            picked = jnp.sum(
                jnp.where(chosen, values[128 * c : 128 * c + 128], 0.0), axis=0, keepdims=True
            )
            fresh = (dual_ref[c, :, span] + (gains * picked - seen_ref[c, :, span])) / 2.0
            dual_out[c, :, span] = fresh
            spread.append(jnp.where(chosen, gains * fresh, 0.0).astype(bf16))
        hold = hold + lax.dot_general(
            jnp.concatenate(spread, axis=0),
            here,
            (((1,), (1,)), ((), ())),
            preferred_element_type=f32,
        )
    held = hold.astype(bf16)
    held = jnp.concatenate(
        [
            jnp.concatenate(
                [held[128 * c + 32 * t : 128 * c + 32 * t + 32] for t in range(4)], axis=1
            )
            for c in range(2)
        ],
        axis=0,
    )
    left = quarters(held[:, :HALF], held[:, HALF:])
    by_cos = whole(dot(left, plain(tables_ref, 0)))
    by_sin = whole(dot(left, plain(tables_ref, 1)))
    pack(by_cos[:32] - by_sin[32:], by_sin[:32] + by_cos[32:], out_ref)


def filtered_columns(values, adjoint):
    rows = values.shape[0]
    padded = jnp.concatenate([values, jnp.zeros((rows, 128), f32)], axis=1)
    even = lax.broadcasted_iota(jnp.int32, (rows, N), 1) % 2 == 0
    total = jnp.zeros((rows, N), f32)
    for shift in range(-4, 5):
        moved = pltpu.roll(padded, (-shift) % (N + 128), 1)[:, :N] if shift else values
        pair = tap_pair(-shift if adjoint else shift)
        if adjoint and shift % 2:
            pair = pair[::-1]
        total = total + moved * jnp.where(even, *pair)
    return total


def exact_dot(a, b, dims):
    return lax.dot_general(
        a, b, (dims, ((), ())), precision=lax.Precision.HIGHEST, preferred_element_type=f32
    )


def wave_kernel(
    margin_ref, image_ref, low_ref, high_ref, coef_ref, square_ref, rows_ref
):
    above = jnp.broadcast_to(low_ref[0:1, 0:48], (48, 48))
    below = jnp.broadcast_to(high_ref[7:8, 0:48], (48, 48))
    rows = row_weights(above, margin_ref[0].astype(f32), below)
    rows_ref[...] = rows
    extended = jnp.concatenate([low_ref[...], image_ref[...], high_ref[...]], axis=0)
    coef = filtered_columns(exact_dot(rows, extended, ((1,), (0,))), False)
    coef_ref[...] = coef
    square_ref[...] = (coef * coef)[:40].astype(bf16)


def join_kernel(parts_ref, out_ref):
    out_ref[...] = jnp.sum(parts_ref[...].astype(f32), axis=0).astype(bf16)


def back_kernel(coef_ref, rows_ref, parts_ref, out_ref):
    total = jnp.sum(parts_ref[...].astype(f32), axis=0)
    factor = bound_level / jnp.maximum(jnp.sqrt(total), bound_level)
    mixed = exact_dot(rows_ref[0:40, :], coef_ref[0:40, :] * factor, ((0,), (0,)))
    out_ref[...] = filtered_columns(mixed[8:40], True)


def final_kernel(got_ref, image_ref, wave_ref, tables_ref, out_ref):
    turned = got_ref[...].reshape(512, 128).T
    real = quarters(*split([turned[:32], turned[32:64]]))
    imag = quarters(*split([turned[64:96], turned[96:]]))
    data = whole(dot(real, regrouped(tables_ref, 0)) - dot(imag, regrouped(tables_ref, 1)))
    total = data + wave_ref[...]
    out_ref[0] = jnp.maximum(image_ref[...] - tau_step * total, 0.0)


in_vmem = pl.BlockSpec(memory_space=pltpu.VMEM)
in_smem = pl.BlockSpec(memory_space=pltpu.SMEM)
in_hbm = pl.BlockSpec(memory_space=pltpu.HBM)


def call(kernel, name, out_shape, *args, specs=None, scratch=(), room=12):
    return pl.pallas_call(
        kernel,
        out_shape=out_shape,
        in_specs=specs or [in_vmem] * len(args),
        out_specs=jax.tree.map(lambda _: in_vmem, out_shape),
        scratch_shapes=list(scratch),
        compiler_params=pltpu.CompilerParams(vmem_limit_bytes=room * 1024 * 1024),
        name=name,
    )(*args)


def shape(dims, kind):
    return jax.ShapeDtypeStruct(dims, kind)


def local(image, margin, cells, weights, observed, dual_start):
    tables = jnp.asarray(fourier_tables())
    chunks = shape((FACETS, 16, 128), bf16)
    squares = shape((40, N), bf16)
    up = [(i, i + 1) for i in range(FACETS - 1)]
    down = [(i + 1, i) for i in range(FACETS - 1)]
    wide = jnp.broadcast_to(margin.astype(f32)[:, None], (1, N))
    low = lax.ppermute(jnp.concatenate([wide, image[0, 25:]], axis=0), "slab", up)
    high = lax.ppermute(jnp.concatenate([image[0, :7], wide], axis=0), "slab", down)
    sent, held, tables_held = call(
        forward_kernel,
        "rows_out",
        (chunks, shape((ROWS, N), f32), shape(tables.shape, bf16)),
        image, tables,
        specs=[in_hbm] * 2,
        scratch=[pltpu.SemaphoreType.DMA, pltpu.SemaphoreType.DMA],
    )
    sent, low, high = lax.optimization_barrier((sent, low, high))
    coef, square, rows = call(
        wave_kernel,
        "wave_out",
        (shape((48, N), f32), squares, shape((48, 48), f32)),
        margin, held, low, high,
        specs=[in_smem] + [in_vmem] * 3,
    )
    got = lax.all_to_all(sent, "slab", 0, 0, tiled=True)
    near = [[c, c + 1, c + 8, c + 9] for c in (0, 2, 4, 6)]
    beside = [[c, c + 2] for c in (0, 1, 4, 5, 8, 9, 12, 13)]
    across = [[c, c + 4] for c in (0, 1, 2, 3, 8, 9, 10, 11)]
    parts = lax.all_gather(square, "chan", axis_index_groups=near)
    part = call(join_kernel, "wave_part", squares, parts)
    got, part = lax.optimization_barrier((got, part))
    dual, back = call(
        vis_kernel,
        "visibilities",
        (shape((2, 1, VIS), f32), chunks),
        got, cells, weights, observed, dual_start, tables_held,
    )
    returned = lax.all_to_all(back, "slab", 0, 0, tiled=True)
    parts = lax.all_gather(part, "chan", axis_index_groups=beside)
    part = call(join_kernel, "wave_more", squares, parts)
    gathered = lax.all_gather(part, "chan", axis_index_groups=across)
    wave = call(back_kernel, "wave_back", shape((ROWS, N), f32), coef, rows, gathered)
    fresh = call(
        final_kernel, "image_out", shape((1, ROWS, N), f32),
        returned, held, wave, tables_held,
    )
    return (fresh, dual)


def solution(mesh):
    in_specs = (
        P("chan", "slab", None),
        P("slab"),
        P("chan", "slab"),
        P("chan", "slab"),
        P(None, "chan", "slab"),
        P(None, "chan", "slab"),
    )
    out_specs = (P("chan", "slab", None), P(None, "chan", "slab"))
    return jax.shard_map(local, mesh=mesh, in_specs=in_specs, out_specs=out_specs, check_vma=False)
```

```python
import math

import jax
import jax.numpy as jnp
import numpy as np
from jax import lax
from jax.experimental import pallas as pl
from jax.experimental.pallas import tpu as pltpu
from jax.sharding import PartitionSpec as P

N = 1024
HALF = 512
ROWS = 32
FACETS = 32
CHANNELS = 16
VIS = 4096
STEP = 512

low_taps = (
    -0.010597401784997278,
    0.032883011666982945,
    0.030841381835986965,
    -0.18703481171888114,
    -0.02798376941698385,
    0.6308807679295904,
    0.7148465705525415,
    0.23037781330885523,
)
high_taps = (
    -0.23037781330885523,
    0.7148465705525415,
    -0.6308807679295904,
    -0.02798376941698385,
    0.18703481171888114,
    0.030841381835986965,
    -0.032883011666982945,
    -0.010597401784997278,
)
tau_step = 0.5
bound_level = 3.0
f32 = jnp.float32
bf16 = jnp.bfloat16


def fourier_tables():
    index = np.arange(HALF, dtype=np.int32)
    product = index[:, None] * index[None, :] % N
    angle = product.astype(np.float32) * np.float32(2.0 * math.pi / N)
    scale = np.float32(1.0 / math.sqrt(N))
    shape = (2, FACETS // 2, 2, 16, HALF)
    pair = np.stack([np.cos(angle) * scale, np.sin(angle) * scale])
    return pair.astype(bf16).reshape(shape)


def tap_pair(shift):
    even = low_taps[shift + 3] if 0 <= shift + 3 < 8 else 0.0
    odd = high_taps[shift + 4] if 0 <= shift + 4 < 8 else 0.0
    return even, odd


def row_weights(above, own, below):
    place = lax.broadcasted_iota(jnp.int32, (48, 48), 0)
    position = place - 4
    line = lax.broadcasted_iota(jnp.int32, (48, 48), 1) - 8
    even = position % 2 == 0
    taps = jnp.zeros((48, 48), f32)
    for shift in range(-4, 5):
        pair = tap_pair(shift)
        taps = jnp.where(line - position == shift, jnp.where(even, *pair), taps)
    inside = jnp.maximum(jnp.maximum(-line, line - ROWS + 1), 0)
    distance = jnp.where(
        place < 4,
        jnp.maximum(line + 1, 0),
        jnp.where(place < 36, inside, jnp.maximum(ROWS - line, 0)),
    )
    width = jnp.where(place < 4, above, jnp.where(place < 36, own, below))
    return jnp.where((distance.astype(f32) <= width) & (place < 40), taps, 0.0)


def exchange_groups(groups):
    lane = lax.broadcasted_iota(jnp.int32, groups[0].shape, 1)
    g = list(groups)
    for width, pairs in ((64, ((0, 2), (1, 3))), (32, ((0, 1), (2, 3)))):
        first = (lane % (2 * width)) < width
        for a, b in pairs:
            x, y = g[a], g[b]
            g[a] = jnp.where(first, x, pltpu.roll(y, width, 1))
            g[b] = jnp.where(first, pltpu.roll(x, 128 - width, 1), y)
    return g


def pack(real, imag, out_ref):
    for block in range(8):
        span = slice(128 * block, 128 * (block + 1))
        groups = [real[:16, span], real[16:, span], imag[:16, span], imag[16:, span]]
        for d, chunk in enumerate(exchange_groups(groups)):
            out_ref[4 * block + d] = chunk.astype(bf16)


def dot(a, b):
    return jnp.dot(a, b, preferred_element_type=f32)


def signs(dims):
    return jnp.where(lax.broadcasted_iota(jnp.int32, dims, 1) % 2 == 0, 1.0, -1.0)


def quarters(low, high):
    sign = signs(low.shape).astype(bf16)
    return jnp.concatenate([low, high, low * sign, high * sign], axis=0)


def whole(products):
    rows = products.shape[0] // 4
    sign = signs((rows, HALF))
    part = [products[rows * t : rows * t + rows] for t in range(4)]
    return jnp.concatenate([part[0] + sign * part[1], part[2] + sign * part[3]], axis=1)


def plain(tables_ref, which):
    return tables_ref[which].reshape(HALF, HALF)


def regrouped(tables_ref, which):
    parts = [tables_ref[which, :, h].reshape(256, HALF) for h in range(2)]
    return jnp.concatenate(parts, axis=0)


def split(pieces):
    return (
        jnp.concatenate([p[:, :256] for p in pieces], axis=1),
        jnp.concatenate([p[:, 256:] for p in pieces], axis=1),
    )


def forward_kernel(image_ref, tables_ref, out_ref, held_ref, tables_out, image_sem, table_sem):
    image_copy = pltpu.make_async_copy(image_ref.at[0], held_ref, image_sem)
    tables_copy = pltpu.make_async_copy(tables_ref, tables_out, table_sem)
    image_copy.start()
    tables_copy.start()
    image_copy.wait()
    flat = held_ref[...].astype(bf16)
    left = quarters(flat[:, :HALF], flat[:, HALF:])
    tables_copy.wait()
    pack(whole(dot(left, plain(tables_out, 0))), -whole(dot(left, plain(tables_out, 1))), out_ref)


def vis_kernel(
    got_ref, parts_ref, cells_ref, gains_ref, seen_ref, dual_ref, tables_ref,
    dual_out, out_ref, part_ref,
):
    part_ref[...] = jnp.sum(parts_ref[...].astype(f32), axis=0).astype(bf16)
    turned = got_ref[...].reshape(512, 128).T
    left = quarters(
        *split(
            [
                jnp.concatenate(
                    [turned[32 * h : 32 * h + 32], turned[64 + 32 * h : 96 + 32 * h]], axis=0
                )
                for h in range(2)
            ]
        )
    )
    by_cos = whole(dot(left, regrouped(tables_ref, 0)))
    by_sin = whole(dot(left, regrouped(tables_ref, 1)))
    grid = (by_cos[:32] + by_sin[32:], by_cos[32:] - by_sin[:32])
    stacked = jnp.concatenate(
        [part[:, 256 * t : 256 * t + 256] for part in grid for t in range(4)], axis=0
    )
    lines = stacked.astype(bf16)
    cell_lane = lax.broadcasted_iota(jnp.int32, (256, STEP), 0).astype(f32).astype(bf16)
    cell_line = lax.broadcasted_iota(jnp.int32, (128, STEP), 0)
    one, zero = jnp.asarray(1.0, bf16), jnp.asarray(0.0, bf16)
    hold = jnp.zeros((256, 256), f32)
    for step in range(VIS // STEP):
        span = slice(STEP * step, STEP * (step + 1))
        cell = cells_ref[:, span]
        lane = cell & 255
        line = ((cell >> 8) & 3) * 32 + (cell >> 10)
        gains = gains_ref[:, span]
        here = jnp.where(cell_lane == lane.astype(f32).astype(bf16), one, zero)
        chosen = cell_line == line
        values = dot(lines, here)
        spread = []
        for c in range(2):
            picked = jnp.sum(
                jnp.where(chosen, values[128 * c : 128 * c + 128], 0.0), axis=0, keepdims=True
            )
            fresh = (dual_ref[c, :, span] + (gains * picked - seen_ref[c, :, span])) / 2.0
            dual_out[c, :, span] = fresh
            spread.append(jnp.where(chosen, gains * fresh, 0.0).astype(bf16))
        hold = hold + lax.dot_general(
            jnp.concatenate(spread, axis=0),
            here,
            (((1,), (1,)), ((), ())),
            preferred_element_type=f32,
        )
    held = hold.astype(bf16)
    held = jnp.concatenate(
        [
            jnp.concatenate(
                [held[128 * c + 32 * t : 128 * c + 32 * t + 32] for t in range(4)], axis=1
            )
            for c in range(2)
        ],
        axis=0,
    )
    left = quarters(held[:, :HALF], held[:, HALF:])
    by_cos = whole(dot(left, plain(tables_ref, 0)))
    by_sin = whole(dot(left, plain(tables_ref, 1)))
    pack(by_cos[:32] - by_sin[32:], by_sin[:32] + by_cos[32:], out_ref)


def filtered_columns(values, adjoint):
    rows = values.shape[0]
    padded = jnp.concatenate([values, jnp.zeros((rows, 128), f32)], axis=1)
    even = lax.broadcasted_iota(jnp.int32, (rows, N), 1) % 2 == 0
    total = jnp.zeros((rows, N), f32)
    for shift in range(-4, 5):
        moved = pltpu.roll(padded, (-shift) % (N + 128), 1)[:, :N] if shift else values
        pair = tap_pair(-shift if adjoint else shift)
        if adjoint and shift % 2:
            pair = pair[::-1]
        total = total + moved * jnp.where(even, *pair)
    return total


def exact_dot(a, b, dims):
    return lax.dot_general(
        a, b, (dims, ((), ())), precision=lax.Precision.HIGHEST, preferred_element_type=f32
    )


def wave_kernel(
    margin_ref, image_ref, first_ref, second_ref, coef_ref, square_ref, rows_ref
):
    first, second = first_ref[...], second_ref[...]
    from_above = jnp.broadcast_to(first[0:1, :], (8, N)) > 0.0
    low = jnp.where(from_above, first, second)
    high = pltpu.roll(jnp.where(from_above, second, first), 7, 0)
    above = jnp.broadcast_to(low[0:1, 0:48], (48, 48))
    below = -jnp.broadcast_to(high[7:8, 0:48], (48, 48))
    rows = row_weights(above, margin_ref[0].astype(f32), below)
    rows_ref[...] = rows
    extended = jnp.concatenate([low, image_ref[...], high], axis=0)
    coef = filtered_columns(exact_dot(rows, extended, ((1,), (0,))), False)
    coef_ref[...] = coef
    square_ref[...] = (coef * coef)[:40].astype(bf16)


def join_kernel(parts_ref, out_ref):
    out_ref[...] = jnp.sum(parts_ref[...].astype(f32), axis=0).astype(bf16)


def final_kernel(got_ref, image_ref, coef_ref, rows_ref, parts_ref, tables_ref, out_ref):
    total = jnp.sum(parts_ref[...].astype(f32), axis=0)
    factor = bound_level / jnp.maximum(jnp.sqrt(total), bound_level)
    mixed = exact_dot(rows_ref[0:40, :], coef_ref[0:40, :] * factor, ((0,), (0,)))
    wave = filtered_columns(mixed[8:40], True)
    turned = got_ref[...].reshape(512, 128).T
    real = quarters(*split([turned[:32], turned[32:64]]))
    imag = quarters(*split([turned[64:96], turned[96:]]))
    data = whole(dot(real, regrouped(tables_ref, 0)) - dot(imag, regrouped(tables_ref, 1)))
    out_ref[0] = jnp.maximum(image_ref[...] - tau_step * (data + wave), 0.0)


in_vmem = pl.BlockSpec(memory_space=pltpu.VMEM)
in_smem = pl.BlockSpec(memory_space=pltpu.SMEM)
in_hbm = pl.BlockSpec(memory_space=pltpu.HBM)


def call(kernel, name, out_shape, *args, specs=None, scratch=(), room=12):
    return pl.pallas_call(
        kernel,
        out_shape=out_shape,
        in_specs=specs or [in_vmem] * len(args),
        out_specs=jax.tree.map(lambda _: in_vmem, out_shape),
        scratch_shapes=list(scratch),
        compiler_params=pltpu.CompilerParams(vmem_limit_bytes=room * 1024 * 1024),
        name=name,
    )(*args)


def shape(dims, kind):
    return jax.ShapeDtypeStruct(dims, kind)


def local(image, margin, cells, weights, observed, dual_start):
    tables = jnp.asarray(fourier_tables())
    chunks = shape((FACETS, 16, 128), bf16)
    squares = shape((40, N), bf16)
    inner = [(i, i ^ 1) for i in range(FACETS)]
    outer = [(i, (i - 1 ^ 1) + 1) for i in range(1, FACETS - 1)]
    wide = jnp.broadcast_to(margin.astype(f32)[:, None], (1, N))
    parity = lax.axis_index("slab") % 2
    bottom = jnp.concatenate([wide, image[0, 25:]], axis=0)
    top = jnp.concatenate([-wide, image[0, :7]], axis=0)
    is_even = parity == 0
    first = lax.ppermute(jnp.where(is_even, bottom, top), "slab", inner)
    second = lax.ppermute(jnp.where(is_even, top, bottom), "slab", outer)
    sent, held, tables_held = call(
        forward_kernel,
        "rows_out",
        (chunks, shape((ROWS, N), f32), shape(tables.shape, bf16)),
        image, tables,
        specs=[in_hbm] * 2,
        scratch=[pltpu.SemaphoreType.DMA, pltpu.SemaphoreType.DMA],
    )
    sent, first, second = lax.optimization_barrier((sent, first, second))
    coef, square, rows = call(
        wave_kernel,
        "wave_out",
        (shape((48, N), f32), squares, shape((48, 48), f32)),
        margin, held, first, second,
        specs=[in_smem] + [in_vmem] * 3,
    )
    got = lax.all_to_all(sent, "slab", 0, 0, tiled=True)
    near = [[c, c + 1, c + 8, c + 9] for c in (0, 2, 4, 6)]
    beside = [[c, c + 2] for c in (0, 1, 4, 5, 8, 9, 12, 13)]
    across = [[c, c + 4] for c in (0, 1, 2, 3, 8, 9, 10, 11)]
    parts = lax.all_gather(square, "chan", axis_index_groups=near)
    dual, back, part = call(
        vis_kernel,
        "visibilities",
        (shape((2, 1, VIS), f32), chunks, squares),
        got, parts, cells, weights, observed, dual_start, tables_held,
    )
    returned = lax.all_to_all(back, "slab", 0, 0, tiled=True)
    parts = lax.all_gather(part, "chan", axis_index_groups=beside)
    part = call(join_kernel, "wave_more", squares, parts)
    gathered = lax.all_gather(part, "chan", axis_index_groups=across)
    fresh = call(
        final_kernel, "image_out", shape((1, ROWS, N), f32),
        returned, held, coef, rows, gathered, tables_held,
    )
    return (fresh, dual)


def solution(mesh):
    in_specs = (
        P("chan", "slab", None),
        P("slab"),
        P("chan", "slab"),
        P("chan", "slab"),
        P(None, "chan", "slab"),
        P(None, "chan", "slab"),
    )
    out_specs = (P("chan", "slab", None), P(None, "chan", "slab"))
    return jax.shard_map(local, mesh=mesh, in_specs=in_specs, out_specs=out_specs, check_vma=False)
```

```python
import math

import jax
import jax.numpy as jnp
import numpy as np
from jax import lax
from jax.experimental import pallas as pl
from jax.experimental.pallas import tpu as pltpu
from jax.sharding import PartitionSpec as P

N = 1024
HALF = 512
ROWS = 32
FACETS = 32
CHANNELS = 16
VIS = 4096
STEP = 256

low_taps = (
    -0.010597401784997278,
    0.032883011666982945,
    0.030841381835986965,
    -0.18703481171888114,
    -0.02798376941698385,
    0.6308807679295904,
    0.7148465705525415,
    0.23037781330885523,
)
high_taps = (
    -0.23037781330885523,
    0.7148465705525415,
    -0.6308807679295904,
    -0.02798376941698385,
    0.18703481171888114,
    0.030841381835986965,
    -0.032883011666982945,
    -0.010597401784997278,
)
tau_step = 0.5
bound_level = 3.0
f32 = jnp.float32
bf16 = jnp.bfloat16


def fourier_tables():
    index = np.arange(HALF, dtype=np.int32)
    product = index[:, None] * index[None, :] % N
    angle = product.astype(np.float32) * np.float32(2.0 * math.pi / N)
    scale = np.float32(1.0 / math.sqrt(N))
    shape = (2, FACETS // 2, 2, 16, HALF)
    pair = np.stack([np.cos(angle) * scale, np.sin(angle) * scale])
    return pair.astype(bf16).reshape(shape)


def tap_pair(shift):
    even = low_taps[shift + 3] if 0 <= shift + 3 < 8 else 0.0
    odd = high_taps[shift + 4] if 0 <= shift + 4 < 8 else 0.0
    return even, odd


def row_weights(above, own, below):
    place = lax.broadcasted_iota(jnp.int32, (48, 48), 0)
    position = place - 4
    line = lax.broadcasted_iota(jnp.int32, (48, 48), 1) - 8
    even = position % 2 == 0
    taps = jnp.zeros((48, 48), f32)
    for shift in range(-4, 5):
        pair = tap_pair(shift)
        taps = jnp.where(line - position == shift, jnp.where(even, *pair), taps)
    inside = jnp.maximum(jnp.maximum(-line, line - ROWS + 1), 0)
    distance = jnp.where(
        place < 4,
        jnp.maximum(line + 1, 0),
        jnp.where(place < 36, inside, jnp.maximum(ROWS - line, 0)),
    )
    width = jnp.where(place < 4, above, jnp.where(place < 36, own, below))
    return jnp.where((distance.astype(f32) <= width) & (place < 40), taps, 0.0)


def exchange_groups(groups):
    lane = lax.broadcasted_iota(jnp.int32, groups[0].shape, 1)
    g = list(groups)
    for width, pairs in ((64, ((0, 2), (1, 3))), (32, ((0, 1), (2, 3)))):
        first = (lane % (2 * width)) < width
        for a, b in pairs:
            x, y = g[a], g[b]
            g[a] = jnp.where(first, x, pltpu.roll(y, width, 1))
            g[b] = jnp.where(first, pltpu.roll(x, 128 - width, 1), y)
    return g


def pack(real, imag, out_ref):
    for block in range(8):
        span = slice(128 * block, 128 * (block + 1))
        groups = [real[:16, span], real[16:, span], imag[:16, span], imag[16:, span]]
        for d, chunk in enumerate(exchange_groups(groups)):
            out_ref[4 * block + d] = chunk.astype(bf16)


def dot(a, b):
    return jnp.dot(a, b, preferred_element_type=f32)


def signs(dims):
    return jnp.where(lax.broadcasted_iota(jnp.int32, dims, 1) % 2 == 0, 1.0, -1.0)


def quarters(low, high):
    sign = signs(low.shape).astype(bf16)
    return jnp.concatenate([low, high, low * sign, high * sign], axis=0)


def whole(products):
    rows = products.shape[0] // 4
    sign = signs((rows, HALF))
    part = [products[rows * t : rows * t + rows] for t in range(4)]
    return jnp.concatenate([part[0] + sign * part[1], part[2] + sign * part[3]], axis=1)


def plain(tables_ref, which):
    return tables_ref[which].reshape(HALF, HALF)


def regrouped(tables_ref, which):
    parts = [tables_ref[which, :, h].reshape(256, HALF) for h in range(2)]
    return jnp.concatenate(parts, axis=0)


def split(pieces):
    return (
        jnp.concatenate([p[:, :256] for p in pieces], axis=1),
        jnp.concatenate([p[:, 256:] for p in pieces], axis=1),
    )


def forward_kernel(image_ref, tables_ref, out_ref, held_ref, tables_out, image_sem, table_sem):
    image_copy = pltpu.make_async_copy(image_ref.at[0], held_ref, image_sem)
    tables_copy = pltpu.make_async_copy(tables_ref, tables_out, table_sem)
    image_copy.start()
    tables_copy.start()
    image_copy.wait()
    flat = held_ref[...].astype(bf16)
    left = quarters(flat[:, :HALF], flat[:, HALF:])
    tables_copy.wait()
    pack(whole(dot(left, plain(tables_out, 0))), -whole(dot(left, plain(tables_out, 1))), out_ref)


def vis_kernel(
    got_ref, parts_ref, cells_ref, gains_ref, seen_ref, dual_ref, tables_ref,
    dual_out, out_ref, part_ref,
):
    part_ref[...] = jnp.sum(parts_ref[...].astype(f32), axis=0).astype(bf16)
    turned = got_ref[...].reshape(512, 128).T
    left = quarters(
        *split(
            [
                jnp.concatenate(
                    [turned[32 * h : 32 * h + 32], turned[64 + 32 * h : 96 + 32 * h]], axis=0
                )
                for h in range(2)
            ]
        )
    )
    by_cos = whole(dot(left, regrouped(tables_ref, 0)))
    by_sin = whole(dot(left, regrouped(tables_ref, 1)))
    grid = (by_cos[:32] + by_sin[32:], by_cos[32:] - by_sin[:32])
    stacked = jnp.concatenate(
        [part[:, 256 * t : 256 * t + 256] for part in grid for t in range(4)], axis=0
    )
    lines = stacked.astype(bf16)
    cell_lane = lax.broadcasted_iota(jnp.int32, (256, STEP), 0).astype(f32).astype(bf16)
    cell_line = lax.broadcasted_iota(jnp.int32, (128, STEP), 0)
    one, zero = jnp.asarray(1.0, bf16), jnp.asarray(0.0, bf16)
    hold = jnp.zeros((256, 256), f32)
    for step in range(VIS // STEP):
        span = slice(STEP * step, STEP * (step + 1))
        cell = cells_ref[:, span]
        lane = cell & 255
        line = ((cell >> 8) & 3) * 32 + (cell >> 10)
        gains = gains_ref[:, span]
        here = jnp.where(cell_lane == lane.astype(f32).astype(bf16), one, zero)
        chosen = cell_line == line
        values = dot(lines, here)
        spread = []
        for c in range(2):
            picked = jnp.sum(
                jnp.where(chosen, values[128 * c : 128 * c + 128], 0.0), axis=0, keepdims=True
            )
            fresh = (dual_ref[c, :, span] + (gains * picked - seen_ref[c, :, span])) / 2.0
            dual_out[c, :, span] = fresh
            spread.append(jnp.where(chosen, gains * fresh, 0.0).astype(bf16))
        hold = hold + lax.dot_general(
            jnp.concatenate(spread, axis=0),
            here,
            (((1,), (1,)), ((), ())),
            preferred_element_type=f32,
        )
    held = hold.astype(bf16)
    held = jnp.concatenate(
        [
            jnp.concatenate(
                [held[128 * c + 32 * t : 128 * c + 32 * t + 32] for t in range(4)], axis=1
            )
            for c in range(2)
        ],
        axis=0,
    )
    left = quarters(held[:, :HALF], held[:, HALF:])
    by_cos = whole(dot(left, plain(tables_ref, 0)))
    by_sin = whole(dot(left, plain(tables_ref, 1)))
    pack(by_cos[:32] - by_sin[32:], by_sin[:32] + by_cos[32:], out_ref)


def filtered_columns(values, adjoint):
    rows = values.shape[0]
    padded = jnp.concatenate([values, jnp.zeros((rows, 128), f32)], axis=1)
    even = lax.broadcasted_iota(jnp.int32, (rows, N), 1) % 2 == 0
    total = jnp.zeros((rows, N), f32)
    for shift in range(-4, 5):
        moved = pltpu.roll(padded, (-shift) % (N + 128), 1)[:, :N] if shift else values
        pair = tap_pair(-shift if adjoint else shift)
        if adjoint and shift % 2:
            pair = pair[::-1]
        total = total + moved * jnp.where(even, *pair)
    return total


def exact_dot(a, b, dims):
    return lax.dot_general(
        a, b, (dims, ((), ())), precision=lax.Precision.HIGHEST, preferred_element_type=f32
    )


def wave_kernel(
    margin_ref, image_ref, first_ref, second_ref, coef_ref, square_ref, rows_ref
):
    first, second = first_ref[...], second_ref[...]
    from_above = jnp.broadcast_to(first[0:1, :], (8, N)) > 0.0
    low = jnp.where(from_above, first, second)
    high = pltpu.roll(jnp.where(from_above, second, first), 7, 0)
    above = jnp.broadcast_to(low[0:1, 0:48], (48, 48))
    below = -jnp.broadcast_to(high[7:8, 0:48], (48, 48))
    rows = row_weights(above, margin_ref[0].astype(f32), below)
    rows_ref[...] = rows
    extended = jnp.concatenate([low, image_ref[...], high], axis=0)
    coef = filtered_columns(exact_dot(rows, extended, ((1,), (0,))), False)
    coef_ref[...] = coef
    square_ref[...] = (coef * coef)[:40].astype(bf16)


def join_kernel(parts_ref, out_ref):
    out_ref[...] = jnp.sum(parts_ref[...].astype(f32), axis=0).astype(bf16)


def final_kernel(got_ref, image_ref, coef_ref, rows_ref, parts_ref, tables_ref, out_ref):
    total = jnp.sum(parts_ref[...].astype(f32), axis=0)
    factor = bound_level / jnp.maximum(jnp.sqrt(total), bound_level)
    mixed = exact_dot(rows_ref[0:40, :], coef_ref[0:40, :] * factor, ((0,), (0,)))
    wave = filtered_columns(mixed[8:40], True)
    turned = got_ref[...].reshape(512, 128).T
    real = quarters(*split([turned[:32], turned[32:64]]))
    imag = quarters(*split([turned[64:96], turned[96:]]))
    data = whole(dot(real, regrouped(tables_ref, 0)) - dot(imag, regrouped(tables_ref, 1)))
    out_ref[0] = jnp.maximum(image_ref[...] - tau_step * (data + wave), 0.0)


in_vmem = pl.BlockSpec(memory_space=pltpu.VMEM)
in_smem = pl.BlockSpec(memory_space=pltpu.SMEM)
in_hbm = pl.BlockSpec(memory_space=pltpu.HBM)


def call(kernel, name, out_shape, *args, specs=None, scratch=(), room=12):
    return pl.pallas_call(
        kernel,
        out_shape=out_shape,
        in_specs=specs or [in_vmem] * len(args),
        out_specs=jax.tree.map(lambda _: in_vmem, out_shape),
        scratch_shapes=list(scratch),
        compiler_params=pltpu.CompilerParams(vmem_limit_bytes=room * 1024 * 1024),
        name=name,
    )(*args)


def shape(dims, kind):
    return jax.ShapeDtypeStruct(dims, kind)


def local(image, margin, cells, weights, observed, dual_start):
    tables = jnp.asarray(fourier_tables())
    chunks = shape((FACETS, 16, 128), bf16)
    squares = shape((40, N), bf16)
    inner = [(i, i ^ 1) for i in range(FACETS)]
    outer = [(i, (i - 1 ^ 1) + 1) for i in range(1, FACETS - 1)]
    wide = jnp.broadcast_to(margin.astype(f32)[:, None], (1, N))
    parity = lax.axis_index("slab") % 2
    bottom = jnp.concatenate([wide, image[0, 25:]], axis=0)
    top = jnp.concatenate([-wide, image[0, :7]], axis=0)
    is_even = parity == 0
    first = lax.ppermute(jnp.where(is_even, bottom, top), "slab", inner)
    second = lax.ppermute(jnp.where(is_even, top, bottom), "slab", outer)
    sent, held, tables_held = call(
        forward_kernel,
        "rows_out",
        (chunks, shape((ROWS, N), f32), shape(tables.shape, bf16)),
        image, tables,
        specs=[in_hbm] * 2,
        scratch=[pltpu.SemaphoreType.DMA, pltpu.SemaphoreType.DMA],
    )
    sent, first, second = lax.optimization_barrier((sent, first, second))
    coef, square, rows = call(
        wave_kernel,
        "wave_out",
        (shape((48, N), f32), squares, shape((48, 48), f32)),
        margin, held, first, second,
        specs=[in_smem] + [in_vmem] * 3,
    )
    got = lax.all_to_all(sent, "slab", 0, 0, tiled=True)
    near = [[c, c + 1, c + 8, c + 9] for c in (0, 2, 4, 6)]
    beside = [[c, c + 2] for c in (0, 1, 4, 5, 8, 9, 12, 13)]
    across = [[c, c + 4] for c in (0, 1, 2, 3, 8, 9, 10, 11)]
    parts = lax.all_gather(square, "chan", axis_index_groups=near)
    dual, back, part = call(
        vis_kernel,
        "visibilities",
        (shape((2, 1, VIS), f32), chunks, squares),
        got, parts, cells, weights, observed, dual_start, tables_held,
    )
    returned = lax.all_to_all(back, "slab", 0, 0, tiled=True)
    parts = lax.all_gather(part, "chan", axis_index_groups=beside)
    part = call(join_kernel, "wave_more", squares, parts)
    gathered = lax.all_gather(part, "chan", axis_index_groups=across)
    fresh = call(
        final_kernel, "image_out", shape((1, ROWS, N), f32),
        returned, held, coef, rows, gathered, tables_held,
    )
    return (fresh, dual)


def solution(mesh):
    in_specs = (
        P("chan", "slab", None),
        P("slab"),
        P("chan", "slab"),
        P("chan", "slab"),
        P(None, "chan", "slab"),
        P(None, "chan", "slab"),
    )
    out_specs = (P("chan", "slab", None), P(None, "chan", "slab"))
    return jax.shard_map(local, mesh=mesh, in_specs=in_specs, out_specs=out_specs, check_vma=False)
```

```python
import math

import jax
import jax.numpy as jnp
import numpy as np
from jax import lax
from jax.experimental import pallas as pl
from jax.experimental.pallas import tpu as pltpu
from jax.sharding import PartitionSpec as P

N = 1024
HALF = 512
ROWS = 32
FACETS = 32
CHANNELS = 16
VIS = 4096
STEP = 256

low_taps = (
    -0.010597401784997278,
    0.032883011666982945,
    0.030841381835986965,
    -0.18703481171888114,
    -0.02798376941698385,
    0.6308807679295904,
    0.7148465705525415,
    0.23037781330885523,
)
high_taps = (
    -0.23037781330885523,
    0.7148465705525415,
    -0.6308807679295904,
    -0.02798376941698385,
    0.18703481171888114,
    0.030841381835986965,
    -0.032883011666982945,
    -0.010597401784997278,
)
tau_step = 0.5
bound_level = 3.0
f32 = jnp.float32
bf16 = jnp.bfloat16


def fourier_tables():
    index = np.arange(HALF, dtype=np.int32)
    product = index[:, None] * index[None, :] % N
    angle = product.astype(np.float32) * np.float32(2.0 * math.pi / N)
    scale = np.float32(1.0 / math.sqrt(N))
    shape = (2, FACETS // 2, 2, 16, HALF)
    pair = np.stack([np.cos(angle) * scale, np.sin(angle) * scale])
    return pair.astype(bf16).reshape(shape)


def tap_pair(shift):
    even = low_taps[shift + 3] if 0 <= shift + 3 < 8 else 0.0
    odd = high_taps[shift + 4] if 0 <= shift + 4 < 8 else 0.0
    return even, odd


def row_weights(above, own, below):
    place = lax.broadcasted_iota(jnp.int32, (48, 48), 0)
    position = place - 4
    line = lax.broadcasted_iota(jnp.int32, (48, 48), 1) - 8
    even = position % 2 == 0
    taps = jnp.zeros((48, 48), f32)
    for shift in range(-4, 5):
        pair = tap_pair(shift)
        taps = jnp.where(line - position == shift, jnp.where(even, *pair), taps)
    inside = jnp.maximum(jnp.maximum(-line, line - ROWS + 1), 0)
    distance = jnp.where(
        place < 4,
        jnp.maximum(line + 1, 0),
        jnp.where(place < 36, inside, jnp.maximum(ROWS - line, 0)),
    )
    width = jnp.where(place < 4, above, jnp.where(place < 36, own, below))
    return jnp.where((distance.astype(f32) <= width) & (place < 40), taps, 0.0)


def exchange_groups(groups):
    lane = lax.broadcasted_iota(jnp.int32, groups[0].shape, 1)
    g = list(groups)
    for width, pairs in ((64, ((0, 2), (1, 3))), (32, ((0, 1), (2, 3)))):
        first = (lane % (2 * width)) < width
        for a, b in pairs:
            x, y = g[a], g[b]
            g[a] = jnp.where(first, x, pltpu.roll(y, width, 1))
            g[b] = jnp.where(first, pltpu.roll(x, 128 - width, 1), y)
    return g


def pack(real, imag, out_ref):
    for block in range(8):
        span = slice(128 * block, 128 * (block + 1))
        groups = [real[:16, span], real[16:, span], imag[:16, span], imag[16:, span]]
        for d, chunk in enumerate(exchange_groups(groups)):
            out_ref[4 * block + d] = chunk.astype(bf16)


def dot(a, b):
    return jnp.dot(a, b, preferred_element_type=f32)


def signs(dims):
    return jnp.where(lax.broadcasted_iota(jnp.int32, dims, 1) % 2 == 0, 1.0, -1.0)


def quarters(low, high):
    sign = signs(low.shape).astype(bf16)
    return jnp.concatenate([low, high, low * sign, high * sign], axis=0)


def whole(products):
    rows = products.shape[0] // 4
    sign = signs((rows, HALF))
    part = [products[rows * t : rows * t + rows] for t in range(4)]
    return jnp.concatenate([part[0] + sign * part[1], part[2] + sign * part[3]], axis=1)


def plain(tables_ref, which):
    return tables_ref[which].reshape(HALF, HALF)


def regrouped(tables_ref, which):
    parts = [tables_ref[which, :, h].reshape(256, HALF) for h in range(2)]
    return jnp.concatenate(parts, axis=0)


def split(pieces):
    return (
        jnp.concatenate([p[:, :256] for p in pieces], axis=1),
        jnp.concatenate([p[:, 256:] for p in pieces], axis=1),
    )


def forward_kernel(image_ref, tables_ref, out_ref):
    flat = image_ref[0].astype(bf16)
    left = quarters(flat[:, :HALF], flat[:, HALF:])
    pack(whole(dot(left, plain(tables_ref, 0))), -whole(dot(left, plain(tables_ref, 1))), out_ref)


def vis_kernel(
    got_ref, parts_ref, cells_ref, gains_ref, seen_ref, dual_ref, tables_ref,
    dual_out, out_ref, part_ref,
):
    part_ref[...] = jnp.sum(parts_ref[...].astype(f32), axis=0).astype(bf16)
    turned = got_ref[...].reshape(512, 128).T
    left = quarters(
        *split(
            [
                jnp.concatenate(
                    [turned[32 * h : 32 * h + 32], turned[64 + 32 * h : 96 + 32 * h]], axis=0
                )
                for h in range(2)
            ]
        )
    )
    by_cos = whole(dot(left, regrouped(tables_ref, 0)))
    by_sin = whole(dot(left, regrouped(tables_ref, 1)))
    grid = (by_cos[:32] + by_sin[32:], by_cos[32:] - by_sin[:32])
    stacked = jnp.concatenate(
        [part[:, 256 * t : 256 * t + 256] for part in grid for t in range(4)], axis=0
    )
    lines = stacked.astype(bf16)
    cell_lane = lax.broadcasted_iota(jnp.int32, (256, STEP), 0).astype(f32).astype(bf16)
    cell_line = lax.broadcasted_iota(jnp.int32, (128, STEP), 0)
    one, zero = jnp.asarray(1.0, bf16), jnp.asarray(0.0, bf16)
    hold = jnp.zeros((256, 256), f32)
    for step in range(VIS // STEP):
        span = slice(STEP * step, STEP * (step + 1))
        cell = cells_ref[:, span]
        lane = cell & 255
        line = ((cell >> 8) & 3) * 32 + (cell >> 10)
        gains = gains_ref[:, span]
        here = jnp.where(cell_lane == lane.astype(f32).astype(bf16), one, zero)
        chosen = cell_line == line
        values = dot(lines, here)
        spread = []
        for c in range(2):
            picked = jnp.sum(
                jnp.where(chosen, values[128 * c : 128 * c + 128], 0.0), axis=0, keepdims=True
            )
            fresh = (dual_ref[c, :, span] + (gains * picked - seen_ref[c, :, span])) / 2.0
            dual_out[c, :, span] = fresh
            spread.append(jnp.where(chosen, gains * fresh, 0.0).astype(bf16))
        hold = hold + lax.dot_general(
            jnp.concatenate(spread, axis=0),
            here,
            (((1,), (1,)), ((), ())),
            preferred_element_type=f32,
        )
    held = hold.astype(bf16)
    held = jnp.concatenate(
        [
            jnp.concatenate(
                [held[128 * c + 32 * t : 128 * c + 32 * t + 32] for t in range(4)], axis=1
            )
            for c in range(2)
        ],
        axis=0,
    )
    left = quarters(held[:, :HALF], held[:, HALF:])
    by_cos = whole(dot(left, plain(tables_ref, 0)))
    by_sin = whole(dot(left, plain(tables_ref, 1)))
    pack(by_cos[:32] - by_sin[32:], by_sin[:32] + by_cos[32:], out_ref)


def filtered_columns(values, adjoint):
    rows = values.shape[0]
    padded = jnp.concatenate([values, jnp.zeros((rows, 128), f32)], axis=1)
    even = lax.broadcasted_iota(jnp.int32, (rows, N), 1) % 2 == 0
    total = jnp.zeros((rows, N), f32)
    for shift in range(-4, 5):
        moved = pltpu.roll(padded, (-shift) % (N + 128), 1)[:, :N] if shift else values
        pair = tap_pair(-shift if adjoint else shift)
        if adjoint and shift % 2:
            pair = pair[::-1]
        total = total + moved * jnp.where(even, *pair)
    return total


def exact_dot(a, b, dims):
    return lax.dot_general(
        a, b, (dims, ((), ())), precision=lax.Precision.HIGHEST, preferred_element_type=f32
    )


def wave_kernel(
    margin_ref, image_ref, first_ref, second_ref, coef_ref, square_ref, rows_ref
):
    first, second = first_ref[...], second_ref[...]
    from_above = jnp.broadcast_to(first[0:1, :], (8, N)) > 0.0
    low = jnp.where(from_above, first, second)
    high = pltpu.roll(jnp.where(from_above, second, first), 7, 0)
    above = jnp.broadcast_to(low[0:1, 0:48], (48, 48))
    below = -jnp.broadcast_to(high[7:8, 0:48], (48, 48))
    rows = row_weights(above, margin_ref[0].astype(f32), below)
    rows_ref[...] = rows
    extended = jnp.concatenate([low, image_ref[0], high], axis=0)
    coef = filtered_columns(exact_dot(rows, extended, ((1,), (0,))), False)
    coef_ref[...] = coef
    square_ref[...] = (coef * coef)[:40].astype(bf16)


def join_kernel(parts_ref, out_ref):
    out_ref[...] = jnp.sum(parts_ref[...].astype(f32), axis=0).astype(bf16)


def final_kernel(got_ref, image_ref, coef_ref, rows_ref, parts_ref, tables_ref, out_ref):
    total = jnp.sum(parts_ref[...].astype(f32), axis=0)
    factor = bound_level / jnp.maximum(jnp.sqrt(total), bound_level)
    mixed = exact_dot(rows_ref[0:40, :], coef_ref[0:40, :] * factor, ((0,), (0,)))
    wave = filtered_columns(mixed[8:40], True)
    turned = got_ref[...].reshape(512, 128).T
    real = quarters(*split([turned[:32], turned[32:64]]))
    imag = quarters(*split([turned[64:96], turned[96:]]))
    data = whole(dot(real, regrouped(tables_ref, 0)) - dot(imag, regrouped(tables_ref, 1)))
    out_ref[0] = jnp.maximum(image_ref[0] - tau_step * (data + wave), 0.0)


in_vmem = pl.BlockSpec(memory_space=pltpu.VMEM)
in_smem = pl.BlockSpec(memory_space=pltpu.SMEM)
in_hbm = pl.BlockSpec(memory_space=pltpu.HBM)


def call(kernel, name, out_shape, *args, specs=None, scratch=(), room=12):
    return pl.pallas_call(
        kernel,
        out_shape=out_shape,
        in_specs=specs or [in_vmem] * len(args),
        out_specs=jax.tree.map(lambda _: in_vmem, out_shape),
        scratch_shapes=list(scratch),
        compiler_params=pltpu.CompilerParams(vmem_limit_bytes=room * 1024 * 1024),
        name=name,
    )(*args)


def shape(dims, kind):
    return jax.ShapeDtypeStruct(dims, kind)


def local(image, margin, cells, weights, observed, dual_start):
    tables = jnp.asarray(fourier_tables())
    chunks = shape((FACETS, 16, 128), bf16)
    squares = shape((40, N), bf16)
    inner = [(i, i ^ 1) for i in range(FACETS)]
    outer = [(i, (i - 1 ^ 1) + 1) for i in range(1, FACETS - 1)]
    wide = jnp.broadcast_to(margin.astype(f32)[:, None], (1, N))
    parity = lax.axis_index("slab") % 2
    bottom = jnp.concatenate([wide, image[0, 25:]], axis=0)
    top = jnp.concatenate([-wide, image[0, :7]], axis=0)
    is_even = parity == 0
    first = lax.ppermute(jnp.where(is_even, bottom, top), "slab", inner)
    second = lax.ppermute(jnp.where(is_even, top, bottom), "slab", outer)
    sent = call(forward_kernel, "rows_out", chunks, image, tables)
    sent, first, second = lax.optimization_barrier((sent, first, second))
    coef, square, rows = call(
        wave_kernel,
        "wave_out",
        (shape((48, N), f32), squares, shape((48, 48), f32)),
        margin, image, first, second,
        specs=[in_smem] + [in_vmem] * 3,
    )
    got = lax.all_to_all(sent, "slab", 0, 0, tiled=True)
    near = [[c, c + 1, c + 8, c + 9] for c in (0, 2, 4, 6)]
    beside = [[c, c + 2] for c in (0, 1, 4, 5, 8, 9, 12, 13)]
    across = [[c, c + 4] for c in (0, 1, 2, 3, 8, 9, 10, 11)]
    parts = lax.all_gather(square, "chan", axis_index_groups=near)
    dual, back, part = call(
        vis_kernel,
        "visibilities",
        (shape((2, 1, VIS), f32), chunks, squares),
        got, parts, cells, weights, observed, dual_start, tables,
    )
    returned = lax.all_to_all(back, "slab", 0, 0, tiled=True)
    parts = lax.all_gather(part, "chan", axis_index_groups=beside)
    part = call(join_kernel, "wave_more", squares, parts)
    gathered = lax.all_gather(part, "chan", axis_index_groups=across)
    fresh = call(
        final_kernel, "image_out", shape((1, ROWS, N), f32),
        returned, image, coef, rows, gathered, tables,
    )
    return (fresh, dual)


def solution(mesh):
    in_specs = (
        P("chan", "slab", None),
        P("slab"),
        P("chan", "slab"),
        P("chan", "slab"),
        P(None, "chan", "slab"),
        P(None, "chan", "slab"),
    )
    out_specs = (P("chan", "slab", None), P(None, "chan", "slab"))
    return jax.shard_map(local, mesh=mesh, in_specs=in_specs, out_specs=out_specs, check_vma=False)
```
